32 devices in a mesh: dp: 8 (over z, y), pix: 4 (over x, core).
Axes of the slice: x: 2, y: 2, z: 4, core: 2. Of those that a mesh axis runs over, the one named last changes fastest.
Arguments:
- latents: bfloat16 [64, 128, 1024], P(('dp', 'pix')), may hold values from -6 to 6
- pixels: bfloat16 [64, 1536, 1024], P('dp', 'pix'), may hold values from -6 to 6
- pixel_mask: int32 [64, 1536], P('dp', 'pix'), may hold values from 0 to 1, as said below
- cotangent: bfloat16 [64, 128, 1024], P(('dp', 'pix')), may hold values from -6 to 6
- lat_gain: float32 [1024], replicated, may hold values from 0.5 to 1.5
- pix_gain: float32 [1024], replicated, may hold values from 0.5 to 1.5
- self_gain: float32 [1024], replicated, may hold values from 0.5 to 1.5
- mlp_gain: float32 [1024], replicated, may hold values from 0.5 to 1.5
- w_query: bfloat16 [1024, 1024], replicated, may hold values from -0.1875 to 0.1875
- w_kv: bfloat16 [1024, 2048], replicated, may hold values from -0.1875 to 0.1875
- w_cross_out: bfloat16 [1024, 1024], replicated, may hold values from -6 to 6
- w_qkv: bfloat16 [1024, 3072], replicated, may hold values from -0.1875 to 0.1875
- w_self_out: bfloat16 [1024, 1024], replicated, may hold values from -1 to 1
- w_mlp_in: bfloat16 [1024, 4096], replicated, may hold values from -0.1875 to 0.1875
- w_mlp_out: bfloat16 [4096, 1024], replicated, may hold values from -0.09375 to 0.09375
Outputs:
- latents_out: bfloat16 [64, 128, 1024], P(('dp', 'pix'))
- d_latents: float32 [64, 128, 1024], P(('dp', 'pix'))
- d_pixels: bfloat16 [64, 1536, 1024], P('dp', 'pix')
- d_lat_gain: float32 [1024], P('dp')
- d_pix_gain: float32 [1024], P('dp')
- d_self_gain: float32 [1024], P('dp')
- d_mlp_gain: float32 [1024], P('dp')
- d_w_query: float32 [1024, 1024], P('dp', 'pix')
- d_w_kv: float32 [1024, 2048], P('dp', 'pix')
- d_w_cross_out: float32 [1024, 1024], P('dp', 'pix')
- d_w_qkv: float32 [1024, 3072], P('dp', 'pix')
- d_w_self_out: float32 [1024, 1024], P('dp', 'pix')
- d_w_mlp_in: float32 [1024, 4096], P('dp', 'pix')
- d_w_mlp_out: float32 [4096, 1024], P('dp', 'pix')
The draws below stay inside these ranges and needn't reach their ends.
Inputs may be any that keep to these rules, and one draw needn't show every extreme that they name: `pixel_mask`: each group's valid pixel slots are its first n, with n one of 474, 929 or 1536; in every aligned block of 8 groups at least one group has all 1536.
All inputs are finite; a program needn't handle non-finite values.
Results may differ from the reference program's by a relative error of at most 0.028.
Values may be sent and summed in bfloat16 or wider, within the bound.
No kernel may reach another device: no remote copies, remote signals or barrier semaphores. Data moves between devices by JAX's collectives and lax.ppermute only.
A program may use at most 320 MiB of HBM per device.

```python
import jax
import jax.numpy as jnp
from jax import lax

D = 1024
FF = 4096
HEADS = 8
L = 128
HD = 128
GROW = 8
GROUPS = 64
P_SIZE = 1536


def draw_pixel_mask(key, part):
    key = jax.random.fold_in(key, 11)
    level_key, spot_key = jax.random.split(key)
    levels = jax.random.randint(level_key, (GROUPS,), 0, 3)
    blocks = GROUPS // GROW
    spot_index = jax.random.randint(spot_key, (blocks,), 0, GROW)
    forced = jnp.arange(GROUPS) % GROW == jnp.repeat(spot_index, GROW)
    levels = jnp.where(forced, 2, levels)
    counts = jnp.where(levels == 0, P_SIZE * 25 // 81, jnp.where(levels == 1, P_SIZE * 49 // 81, P_SIZE))
    return (jnp.arange(P_SIZE)[None, :] < counts[:, None]).astype(jnp.int32)


def block_levels(key, shape, cuts, low, top_value):
    factor_of = 1.0
    for dim, parts in cuts:
        steps = jax.random.uniform(jax.random.fold_in(jax.random.fold_in(key, 6), dim), (parts,), jnp.float32, low / len(cuts), top_value / len(cuts))
        factor_of = factor_of * jnp.repeat(jnp.exp(steps), shape[dim] // parts).reshape((-1,) + (1,) * (len(shape) - 1 - dim))
    return factor_of


def scatter_about(rng, shape, spread, reach, cuts=(), kind=jnp.bfloat16):
    array = spread * jax.random.normal(rng, shape, jnp.float32)
    if cuts:
        array = array * block_levels(rng, shape, cuts, -0.22, 0.18)
    return jnp.clip(array, -reach, reach).astype(kind)


def setup_inputs(seed: int = 0) -> dict:
    keys = jax.random.split(jax.random.key(seed), 16)
    return {
        "latents": scatter_about(keys[0], (GROUPS, L, D), 1.0, 6.0, ((0, 32),)),
        "pixels": scatter_about(keys[1], (GROUPS, P_SIZE, D), 1.0, 6.0, ((0, 8), (1, 4))),
        "pixel_mask": draw_pixel_mask(jax.random.fold_in(keys[15], 71), 0),
        "cotangent": scatter_about(keys[3], (GROUPS, L, D), 1.0, 6.0, ((0, 32),)),
        "lat_gain": jnp.clip(1.0 + 0.1 * jax.random.normal(keys[4], (D,), jnp.float32), 0.5, 1.5),
        "pix_gain": jnp.clip(1.0 + 0.1 * jax.random.normal(keys[5], (D,), jnp.float32), 0.5, 1.5),
        "self_gain": jnp.clip(1.0 + 0.1 * jax.random.normal(keys[6], (D,), jnp.float32), 0.5, 1.5),
        "mlp_gain": jnp.clip(1.0 + 0.1 * jax.random.normal(keys[7], (D,), jnp.float32), 0.5, 1.5),
        "w_query": scatter_about(keys[8], (D, D), D ** -0.5, 0.1875),
        "w_kv": scatter_about(keys[9], (D, 2 * D), D ** -0.5, 0.1875),
        "w_cross_out": scatter_about(keys[10], (D, D), 1 ** -0.5, 6.0),
        "w_qkv": scatter_about(keys[11], (D, 3 * D), D ** -0.5, 0.1875),
        "w_self_out": scatter_about(keys[12], (D, D), (L // 4) ** -0.5, 1.0),
        "w_mlp_in": scatter_about(keys[13], (D, FF), D ** -0.5, 0.1875),
        "w_mlp_out": scatter_about(keys[14], (FF, D), FF ** -0.5, 0.09375),
    }


@jax.custom_vjp
def low(v):
    return lax.optimization_barrier(v.astype(jnp.bfloat16)).astype(jnp.float32)

@jax.custom_vjp
def low_back(v):
    return v

def low_keep(v):
    return (low(v), None)

def low_pass(kept, grad):
    return (grad,)

def back_keep(v):
    return (v, None)

def back_low(kept, grad):
    return (low(grad),)
low.defvjp(low_keep, low_pass)
low_back.defvjp(back_keep, back_low)
EPSILON = 1e-05

def layer_norm(values_in, norm_gain):
    row_mean = lax.optimization_barrier(jnp.mean(values_in, axis=-1, keepdims=True))
    centred = values_in - row_mean
    row_var = lax.optimization_barrier(jnp.mean(centred * centred, axis=-1, keepdims=True))
    return centred * lax.rsqrt(row_var + EPSILON) * norm_gain

def matmul(left_rows, right_rows):
    return jnp.dot(left_rows, right_rows, precision=lax.Precision.HIGHEST, preferred_element_type=jnp.float32)

def attend(query_rows, key_rows, value_rows, valid_mask):
    row_count = query_rows.shape[0]
    query_heads = query_rows.reshape(row_count, HEADS, HD)
    key_heads = key_rows.reshape(key_rows.shape[0], HEADS, HD)
    value_heads = value_rows.reshape(value_rows.shape[0], HEADS, HD)
    scores = low_back(jnp.einsum('lhd,phd->hlp', query_heads, key_heads, precision=lax.Precision.HIGHEST) * HD ** (-0.5))
    masked = jnp.where(valid_mask[None, None, :] > 0, scores, -1e+30)
    row_top = lax.optimization_barrier(jnp.max(masked, axis=-1, keepdims=True))
    expo_rows = jnp.exp(masked - row_top) * valid_mask[None, None, :]
    weights = low(expo_rows / lax.optimization_barrier(jnp.sum(expo_rows, axis=-1, keepdims=True)))
    mixed_heads = jnp.einsum('hlp,phd->lhd', weights, value_heads, precision=lax.Precision.HIGHEST)
    return mixed_heads.reshape(row_count, HEADS * HD)

def group_forward(params, latent, pixel_rows, valid_mask):
    lat_gain, pix_gain, self_gain, mlp_gain, w_query, w_kv, w_cross_out, w_qkv, w_self_out, w_mlp_in, w_mlp_out = params
    lat_normed = low(layer_norm(latent, lat_gain))
    query_rows = low_back(low(matmul(lat_normed, w_query)))
    pix_normed = low(layer_norm(pixel_rows, pix_gain))
    key_value = low_back(low(matmul(pix_normed, w_kv)))
    cross_mixed = low_back(low(attend(query_rows, key_value[:, :D], key_value[:, D:], valid_mask)))
    first_sum = latent + low_back(matmul(cross_mixed, w_cross_out))
    self_normed = low(layer_norm(first_sum, self_gain))
    self_qkv = low_back(low(matmul(self_normed, w_qkv)))
    inner_mixed = low_back(low(attend(self_qkv[:, :D], self_qkv[:, D:2 * D], self_qkv[:, 2 * D:], jnp.ones((L,), jnp.float32))))
    second = first_sum + low_back(matmul(inner_mixed, w_self_out))
    mlp_normed = low(layer_norm(second, mlp_gain))
    hidden = low_back(matmul(mlp_normed, w_mlp_in))
    activation = low(jax.nn.gelu(hidden, approximate=False))
    return second + low_back(matmul(activation, w_mlp_out))

def reference(latents, pixels, pixel_mask, cotangent, lat_gain, pix_gain, self_gain, mlp_gain, w_query, w_kv, w_cross_out, w_qkv, w_self_out, w_mlp_in, w_mlp_out):
    params = tuple((weight.astype(jnp.float32) for weight in (lat_gain, pix_gain, self_gain, mlp_gain, w_query, w_kv, w_cross_out, w_qkv, w_self_out, w_mlp_in, w_mlp_out)))
    lat_float = latents.astype(jnp.float32)
    pix_float = pixels.astype(jnp.float32)
    valid_float = pixel_mask.astype(jnp.float32)

    def forward(param_set, lat_in, pix_in):
        group_step = jax.checkpoint(lambda packed: group_forward(param_set, packed[0], packed[1], packed[2]))
        return lax.map(group_step, (lat_in, pix_in, valid_float))
    result, pullback = jax.vjp(forward, params, lat_float, pix_float)
    param_grads, d_lat, d_pix = pullback(cotangent.astype(jnp.float32))
    return (result.astype(jnp.bfloat16), d_lat, d_pix.astype(jnp.bfloat16), param_grads[0], param_grads[1], param_grads[2], param_grads[3], param_grads[4], param_grads[5], param_grads[6], param_grads[7], param_grads[8], param_grads[9], param_grads[10])
```

```python
import functools

import jax
import jax.numpy as jnp
from jax import lax
from jax.experimental import pallas as pl
from jax.experimental.pallas import tpu as pltpu
from jax.sharding import PartitionSpec as P

HEADS = 8
EPSILON = 1e-05
LANES = 128
EMPTY = -1e30
F32 = jnp.float32
BF16 = jnp.bfloat16
NN = (((1,), (0,)), ((), ()))
NT = (((1,), (1,)), ((), ()))
TN = (((0,), (0,)), ((), ()))
ANY = pl.BlockSpec(memory_space=pl.ANY)
MIB = 1024 * 1024


def grid_sizes():
    pix_size = lax.axis_size("pix")
    dp_size = lax.axis_size("dp")
    slow = 4 if dp_size % 4 == 0 else 1
    return {"c": 2, "x": pix_size // 2, "a": slow, "b": dp_size // slow}


def direction(label):
    axis = "pix" if label in "cx" else "dp"
    here = lax.axis_index(axis)
    inner = 2 if axis == "pix" else grid_sizes()["b"]
    if label in "cb":
        return axis, lax.rem(here, inner), 1
    return axis, here // inner, inner


def move(value, label, moves):
    sizes = grid_sizes()
    axis, _, stride = direction(label)
    other = {"c": "x", "x": "c", "a": "b", "b": "a"}[label]
    other_stride = sizes[label] if stride == 1 else 1
    pairs = [
        (src * stride + rest * other_stride, dst * stride + rest * other_stride)
        for rest in range(sizes[other])
        for src, dst in moves
    ]
    return lax.ppermute(value, axis, pairs)


def from_core(value):
    return move(value, "c", [(0, 1), (1, 0)])


def from_x(value, turn):
    size = grid_sizes()["x"]
    return move(value, "x", [((p + turn) % size, p) for p in range(size)])


def add_low(*terms):
    total = terms[0].astype(F32)
    for term in terms[1:]:
        total = total + term.astype(F32)
    return total.astype(terms[0].dtype)


def take_part(parts, index):
    return lax.dynamic_index_in_dim(parts, index, 0, keepdims=False)


def chain_reduce(parts, label):
    size = grid_sizes()[label]
    if size == 1:
        return parts[0]
    _, here, _ = direction(label)
    mine = take_part(parts, here)
    if size == 2:
        return add_low(mine, move(take_part(parts, 1 - here), label, [(0, 1), (1, 0)]))
    up = down = None
    for step in range(1, size):
        up_own = take_part(parts, jnp.clip(size - step + here, 0, size - 1))
        down_own = take_part(parts, jnp.clip(here - (size - step), 0, size - 1))
        up_sent = up_own if up is None else add_low(up_own, up)
        down_sent = down_own if down is None else add_low(down_own, down)
        up = move(up_sent, label, [(p, p + 1) for p in range(step)])
        down = move(down_sent, label, [(size - 1 - p, size - 2 - p) for p in range(step)])
    return add_low(mine, up, down)


def reduce_parts(parts, order):
    for label in order:
        parts = chain_reduce(parts, label)
    return parts.astype(F32)


def everywhere(value, label):
    size = grid_sizes()[label]
    total = value
    for turn in range(1, size):
        total = total + move(value, label, [(p, (p + turn) % size) for p in range(size)])
    return total


def reduce_gains(grads):
    sizes = grid_sizes()
    parts = grads.reshape(grads.shape[0], sizes["a"], sizes["b"], -1).transpose(2, 1, 0, 3)
    total = chain_reduce(chain_reduce(parts, "b"), "a")
    return everywhere(everywhere(total, "c"), "x")


def dot(left, right, dims=NN):
    return lax.dot_general(left, right, dims, preferred_element_type=F32)


def normalize(values):
    centred = values - jnp.mean(values, axis=-1, keepdims=True)
    root = lax.rsqrt(jnp.mean(centred * centred, axis=-1, keepdims=True) + EPSILON)
    return centred * root, root


def norm_low(values, gain):
    return (normalize(values)[0] * gain).astype(BF16)


def norm_back(values, gain, grad):
    hat, root = normalize(values)
    scaled = grad * gain
    along = jnp.mean(scaled * hat, axis=-1, keepdims=True)
    back = root * (scaled - jnp.mean(scaled, axis=-1, keepdims=True) - hat * along)
    parts = grad * hat
    return back, parts.reshape(parts.shape[0] // 8, 8, parts.shape[1]).sum(0)


def pack_stat(stat):
    lane = lax.broadcasted_iota(jnp.int32, stat.shape, 1)
    high = stat.astype(BF16).astype(F32)
    middle = (stat - high).astype(BF16).astype(F32)
    low = stat - high - middle
    packed = jnp.where(lane < HEADS, high, pltpu.roll(middle, HEADS, 1))
    packed = jnp.where(lane < 2 * HEADS, packed, pltpu.roll(low, 2 * HEADS, 1))
    return jnp.where(lane < 3 * HEADS, packed, 0.0)


def unpack_stat(packed):
    full = packed.astype(F32)
    return (
        full + pltpu.roll(full, LANES - HEADS, 1) + pltpu.roll(full, LANES - 2 * HEADS, 1)
    )


def head(index, base=0):
    return slice(base + index * LANES, base + (index + 1) * LANES)


def merge(first, second, width):
    first_stat = unpack_stat(first[:, width:])
    second_stat = unpack_stat(second[:, width:])
    top = jnp.maximum(first_stat, second_stat)
    first_weight = jnp.exp(first_stat - top)
    second_weight = jnp.exp(second_stat - top)
    total = first_weight + second_weight
    first_weight = first_weight / total
    second_weight = second_weight / total
    mixed = [
        first[:, head(h)].astype(F32) * first_weight[:, h : h + 1]
        + second[:, head(h)].astype(F32) * second_weight[:, h : h + 1]
        for h in range(HEADS)
    ]
    return mixed, top + jnp.log(total)


def params(limit=56):
    return pltpu.CompilerParams(vmem_limit_bytes=limit * MIB)


def cost(flops, moved, exps=0):
    return pl.CostEstimate(flops=int(flops), bytes_accessed=int(moved), transcendentals=int(exps))


def shape_of(shape, dtype):
    return jax.ShapeDtypeStruct(shape, dtype)


def pix_project_kernel(pix_ref, gain_ref, weight_ref, low_ref, kv_ref):
    low = norm_low(pix_ref[...].astype(F32), gain_ref[...])
    low_ref[...] = low
    kv_ref[...] = dot(low, weight_ref[...]).astype(BF16)


def pix_project(pixels, gain, weight):
    rows, width = pixels.shape
    wide = weight.shape[1]
    block = 384 if rows % 384 == 0 else 128
    return pl.pallas_call(
        pix_project_kernel,
        grid=(rows // block,),
        in_specs=[
            pl.BlockSpec((block, width), lambda i: (i, 0)),
            pl.BlockSpec((1, width), lambda i: (0, 0)),
            pl.BlockSpec((width, wide), lambda i: (0, 0)),
        ],
        out_specs=[
            pl.BlockSpec((block, width), lambda i: (i, 0)),
            pl.BlockSpec((block, wide), lambda i: (i, 0)),
        ],
        out_shape=[shape_of((rows, width), BF16), shape_of((rows, wide), BF16)],
        compiler_params=params(),
        cost_estimate=cost(2 * rows * width * wide, 2 * rows * (2 * width + wide)),
        name="pix_project",
    )(pixels, gain, weight)


def cross_forward_kernel(group_ref, count_ref, query_ref, kv_ref, out_ref):
    count = count_ref[group_ref[pl.program_id(0)]]
    rows, width = query_ref.shape[1:]
    slots = kv_ref.shape[1]
    valid = lax.broadcasted_iota(jnp.int32, (1, slots), 1) < count
    lane = lax.broadcasted_iota(jnp.int32, (rows, LANES), 1)
    stat = jnp.zeros((rows, LANES), F32)
    for h in range(HEADS):
        scores = dot(query_ref[0, :, head(h)], kv_ref[0, :, head(h)], NT) * LANES**-0.5
        scores = jnp.where(valid, scores, EMPTY)
        top = jnp.max(scores, axis=-1, keepdims=True)
        expo = jnp.where(valid, jnp.exp(scores - top), 0.0)
        total = jnp.sum(expo, axis=-1, keepdims=True)
        mixed = dot(expo.astype(BF16), kv_ref[0, :, head(h, width)])
        some = total > 0.0
        safe = jnp.where(some, total, 1.0)
        out_ref[0, :, head(h)] = (mixed / safe).astype(BF16)
        stat = jnp.where(lane == h, jnp.where(some, top + jnp.log(safe), EMPTY), stat)
    out_ref[0, :, width:] = pack_stat(stat).astype(BF16)


def cross_forward(groups, counts, query, kv):
    number, rows, width = query.shape
    slots, wide = kv.shape[1:]
    return pl.pallas_call(
        cross_forward_kernel,
        grid_spec=pltpu.PrefetchScalarGridSpec(
            num_scalar_prefetch=2,
            grid=(number,),
            in_specs=[
                pl.BlockSpec((1, rows, width), lambda i, g, n: (i, 0, 0)),
                pl.BlockSpec((1, slots, wide), lambda i, g, n: (g[i], 0, 0)),
            ],
            out_specs=pl.BlockSpec((1, rows, width + LANES), lambda i, g, n: (i, 0, 0)),
        ),
        out_shape=shape_of((number, rows, width + LANES), BF16),
        compiler_params=params(),
        cost_estimate=cost(
            8 * number * rows * width * slots, 2 * number * slots * wide, number * rows * HEADS * slots
        ),
        name="cross_forward",
    )(groups, counts, query, kv)


def merge_kernel(first_ref, second_ref, out_ref):
    width = out_ref.shape[2] - LANES
    mixed, stat = merge(first_ref[0], second_ref[0], width)
    for h in range(HEADS):
        out_ref[0, :, head(h)] = mixed[h].astype(BF16)
    out_ref[0, :, width:] = pack_stat(stat).astype(BF16)


def merge_call(first, second):
    number, rows, wide = first.shape
    spec = pl.BlockSpec((1, rows, wide), lambda i: (i, 0, 0))
    return pl.pallas_call(
        merge_kernel,
        grid=(number,),
        in_specs=[spec, spec],
        out_specs=spec,
        out_shape=shape_of(first.shape, BF16),
        compiler_params=params(),
        cost_estimate=cost(8 * number * rows * wide, 6 * number * rows * wide),
        name="merge",
    )(first, second)


def cross_backward_kernel(group_ref, count_ref, query_ref, grad_ref, kv_ref, old_ref, dq_ref, dkv_ref):
    del old_ref
    count = count_ref[group_ref[pl.program_id(0)]]
    width = query_ref.shape[2]
    slots = kv_ref.shape[1]
    valid = lax.broadcasted_iota(jnp.int32, (slots, 1), 0) < count
    stat = grad_ref[0, :, width:].astype(F32).T
    pieces = [stat[HEADS * i : HEADS * (i + 1)] for i in range(6)]
    log_total = pieces[0] + pieces[1] + pieces[2]
    delta = pieces[3] + pieces[4] + pieces[5]
    scale = LANES**-0.5
    for h in range(HEADS):
        query = query_ref[0, :, head(h)]
        grad = grad_ref[0, :, head(h)]
        keys = kv_ref[0, :, head(h)]
        scores = dot(keys, query, NT) * scale - log_total[h : h + 1]
        probs = jnp.where(valid, jnp.exp(scores), 0.0)
        d_probs = dot(kv_ref[0, :, head(h, width)], grad, NT)
        d_scores = (probs * (d_probs - delta[h : h + 1])).astype(BF16)
        dkv_ref[0, :, head(h)] = (dot(d_scores, query) * scale).astype(BF16)
        dkv_ref[0, :, head(h, width)] = dot(probs.astype(BF16), grad).astype(BF16)
        dq_ref[0, :, head(h)] = (dot(d_scores, keys, TN) * scale).astype(BF16)


def cross_backward(groups, counts, query, grad, kv, old):
    number, rows, width = query.shape
    slots, wide = kv.shape[1:]
    first = old is None
    return pl.pallas_call(
        cross_backward_kernel,
        grid_spec=pltpu.PrefetchScalarGridSpec(
            num_scalar_prefetch=2,
            grid=(number,),
            in_specs=[
                pl.BlockSpec((1, rows, width), lambda i, g, n: (i, 0, 0)),
                pl.BlockSpec((1, rows, width + LANES), lambda i, g, n: (i, 0, 0)),
                pl.BlockSpec((1, slots, wide), lambda i, g, n: (g[i], 0, 0)),
                ANY,
            ],
            out_specs=[
                pl.BlockSpec((1, rows, width), lambda i, g, n: (i, 0, 0)),
                pl.BlockSpec((1, slots, wide), lambda i, g, n: (g[i], 0, 0)),
            ],
        ),
        out_shape=[shape_of((number, rows, width), BF16), shape_of(kv.shape, BF16)],
        input_output_aliases={} if first else {5: 1},
        compiler_params=params(),
        cost_estimate=cost(
            10 * number * rows * width * slots, 4 * number * slots * wide, number * rows * HEADS * slots
        ),
        name="cross_backward",
    )(groups, counts, query, grad, kv, counts if first else old)


def pix_back_kernel(dkv_ref, weight_ref, pix_ref, gain_ref, out_ref, sum_ref):
    back, sums = norm_back(
        pix_ref[...].astype(F32), gain_ref[...], dot(dkv_ref[...], weight_ref[...], NT)
    )
    out_ref[...] = back.astype(BF16)

    @pl.when(pl.program_id(0) == 0)
    def _():
        sum_ref[...] = jnp.zeros_like(sum_ref)

    sum_ref[...] += sums


def pix_back(dkv, weight, pixels, gain):
    rows, width = pixels.shape
    wide = weight.shape[1]
    block = 384 if rows % 384 == 0 else 128
    return pl.pallas_call(
        pix_back_kernel,
        grid=(rows // block,),
        in_specs=[
            pl.BlockSpec((block, wide), lambda i: (i, 0)),
            pl.BlockSpec((width, wide), lambda i: (0, 0)),
            pl.BlockSpec((block, width), lambda i: (i, 0)),
            pl.BlockSpec((1, width), lambda i: (0, 0)),
        ],
        out_specs=[
            pl.BlockSpec((block, width), lambda i: (i, 0)),
            pl.BlockSpec((8, width), lambda i: (0, 0)),
        ],
        out_shape=[shape_of((rows, width), BF16), shape_of((8, width), F32)],
        compiler_params=params(),
        cost_estimate=cost(2 * rows * width * wide, 2 * rows * (2 * width + wide)),
        name="pix_back",
    )(dkv, weight, pixels, gain)


def block_index(order, **at):
    return tuple(at[label] for label in order)


def weight_half_kernel(order, sizes, number, *refs):
    lefts = refs[1 : 1 + number]
    rights = refs[1 + number : 1 + 2 * number]
    other = refs[1 + 2 * number] if len(refs) == 3 + 2 * number else None
    out_ref = refs[-1]
    begin = 0
    for left, right in zip(lefts, rights):
        grad = dot(left[...], right[...], TN)
        end = begin + grad.shape[1]
        rows = grad.shape[0] // (sizes["a"] * sizes["b"])
        for a in range(sizes["a"]):
            for b in range(sizes["b"]):
                at = block_index(order, x=0, a=a, b=b)
                spot = a * sizes["b"] + b
                part = grad[spot * rows : (spot + 1) * rows]
                if other is not None:
                    part = part + other[at + (slice(None), slice(begin, end))].astype(F32)
                out_ref[at + (slice(None), slice(begin, end))] = part.astype(BF16)
        begin = end


def weight_half(pairs, half, other, order):
    sizes = grid_sizes()
    blocks = 2 * sizes["x"]
    depth, tall = pairs[0][0].shape
    widths = [right.shape[1] // blocks for _, right in pairs]
    rows = tall // (sizes["a"] * sizes["b"])
    full = tuple(sizes[label] for label in order) + (rows, sum(widths))
    part = tuple(1 if label == "x" else sizes[label] for label in order) + (rows, sum(widths))

    def spot(i, h):
        return tuple(i if label == "x" else 0 for label in order) + (0, 0)

    out_spec = pl.BlockSpec(part, spot)
    others = [] if other is None else [other]
    moved = 2 * tall * sum(widths) * sizes["x"] * (1 + len(others))
    return pl.pallas_call(
        functools.partial(weight_half_kernel, order, sizes, len(pairs)),
        grid_spec=pltpu.PrefetchScalarGridSpec(
            num_scalar_prefetch=1,
            grid=(sizes["x"],),
            in_specs=[pl.BlockSpec((depth, tall), lambda i, h: (0, 0)) for _ in pairs]
            + [pl.BlockSpec((depth, w), lambda i, h: (0, 2 * i + h[0])) for w in widths]
            + [out_spec for _ in others],
            out_specs=out_spec,
        ),
        out_shape=shape_of(full, BF16),
        compiler_params=params(),
        cost_estimate=cost(2 * depth * tall * sum(widths) * sizes["x"], moved),
        name="weight_half",
    )(half, *[left for left, _ in pairs], *[right for _, right in pairs], *others)


def pix_weight_kernel(order, sizes, *refs):
    left_ref = refs[1]
    rights = refs[2 : 2 + sizes["x"]]
    others = refs[2 + sizes["x"] : -2]
    out_ref, total_ref = refs[-2:]
    step = pl.program_id(0)
    left = left_ref[...]
    for x in range(sizes["x"]):
        grad = dot(left, rights[x][...], TN)

        @pl.when(step == 0)
        def _():
            total_ref[x] = grad

        @pl.when(step > 0)
        def _():
            total_ref[x] += grad

    @pl.when(step == pl.num_programs(0) - 1)
    def _():
        rows = left_ref.shape[1] // (sizes["a"] * sizes["b"])
        for x in range(sizes["x"]):
            for a in range(sizes["a"]):
                for b in range(sizes["b"]):
                    at = block_index(order, x=x, a=a, b=b)
                    spot = a * sizes["b"] + b
                    part = total_ref[x, spot * rows : (spot + 1) * rows]
                    for other in others:
                        part = part + other[at].astype(F32)
                    out_ref[at] = part.astype(BF16)


def pix_weight_half(left, right, half, other, order):
    sizes = grid_sizes()
    depth, tall = left.shape
    width = right.shape[1] // (2 * sizes["x"])
    rows = tall // (sizes["a"] * sizes["b"])
    full = tuple(sizes[label] for label in order) + (rows, width)
    others = [] if other is None else [other]
    block = 768 if depth % 768 == 0 else 128
    whole = pl.BlockSpec(full, lambda i, h: (0,) * len(full))
    return pl.pallas_call(
        functools.partial(pix_weight_kernel, order, sizes),
        grid_spec=pltpu.PrefetchScalarGridSpec(
            num_scalar_prefetch=1,
            grid=(depth // block,),
            in_specs=[pl.BlockSpec((block, tall), lambda i, h: (i, 0))]
            + [
                pl.BlockSpec((block, width), lambda i, h, x=x: (i, 2 * x + h[0]))
                for x in range(sizes["x"])
            ]
            + [whole for _ in others],
            out_specs=whole,
            scratch_shapes=[pltpu.VMEM((sizes["x"], tall, width), F32)],
        ),
        out_shape=shape_of(full, BF16),
        compiler_params=params(),
        cost_estimate=cost(2 * depth * tall * width * sizes["x"], 2 * depth * (tall + width)),
        name="pix_weight_half",
    )(half, left, *[right for _ in range(sizes["x"])], *others)


def start_loads(sources, targets, sems):
    copies = [
        pltpu.make_async_copy(source, target, sems.at[i])
        for i, (source, target) in enumerate(zip(sources, targets))
    ]
    for copy in copies:
        copy.start()
    return copies


def self_softmax(query, keys):
    scores = dot(query, keys, NT) * LANES**-0.5
    expo = jnp.exp(scores - jnp.max(scores, axis=-1, keepdims=True))
    return expo / jnp.sum(expo, axis=-1, keepdims=True)


def latent_forward_kernel(
    group_rows,
    part_count,
    *refs,
):
    parts = refs[:part_count]
    (
        lat_ref,
        d_act_ref,
        self_gain_ref,
        mlp_gain_ref,
        w_cross_hbm,
        w_qkv_hbm,
        w_self_hbm,
        w_in_hbm,
        cross_ref,
        stat_ref,
        first_ref,
        self_low_ref,
        qkv_ref,
        inner_ref,
        second_ref,
        mlp_low_ref,
        act_ref,
        d_hidden_ref,
        w_cross,
        w_qkv,
        w_self,
        w_in,
        sems,
    ) = refs[part_count:]
    loads = start_loads(
        (w_cross_hbm, w_qkv_hbm, w_self_hbm, w_in_hbm), (w_cross, w_qkv, w_self, w_in), sems
    )
    rows, width = lat_ref.shape
    if part_count == 1:
        cross_ref[...] = parts[0][:, :width]
        stat_ref[...] = unpack_stat(parts[0][:, width:])
    else:
        joined = parts[0][...]
        for i, part in enumerate(parts[1:]):
            mixed, stat = merge(joined, part[...], width)
            if i < part_count - 2:
                joined = jnp.concatenate(
                    [m.astype(BF16) for m in mixed] + [pack_stat(stat).astype(BF16)], axis=1
                )
        for h in range(HEADS):
            cross_ref[:, head(h)] = mixed[h].astype(BF16)
        stat_ref[...] = stat
    loads[0].wait()
    first = lat_ref[...].astype(F32) + dot(cross_ref[...], w_cross[...])
    first_ref[...] = first
    self_low_ref[...] = norm_low(first, self_gain_ref[...])
    loads[1].wait()
    for part in range(3):
        cols = slice(part * width, (part + 1) * width)
        qkv_ref[:, cols] = dot(self_low_ref[...], w_qkv[:, cols]).astype(BF16)
    for g in range(rows // group_rows):
        at = slice(g * group_rows, (g + 1) * group_rows)
        for h in range(HEADS):
            probs = self_softmax(qkv_ref[at, head(h)], qkv_ref[at, head(h, width)])
            inner_ref[at, head(h)] = dot(
                probs.astype(BF16), qkv_ref[at, head(h, 2 * width)]
            ).astype(BF16)
    loads[2].wait()
    second = first_ref[...] + dot(inner_ref[...], w_self[...])
    second_ref[...] = second
    mlp_low_ref[...] = norm_low(second, mlp_gain_ref[...])
    loads[3].wait()
    chunk = 512

    def step(i, carry):
        cols = pl.ds(pl.multiple_of(i * chunk, chunk), chunk)
        hidden = dot(mlp_low_ref[...], w_in[:, cols])
        gate = 0.5 + 0.5 * lax.erf(hidden * 0.5**0.5)
        bell = jnp.exp(-0.5 * hidden * hidden) * 0.3989422804014327
        act_ref[:, cols] = (hidden * gate).astype(BF16)
        d_hidden_ref[:, cols] = (d_act_ref[:, cols] * (gate + hidden * bell)).astype(BF16)
        return carry

    lax.fori_loop(0, w_in.shape[1] // chunk, step, 0)


def latent_forward(parts, group_rows, latents, d_act, self_gain, mlp_gain, weights):
    rows, width = latents.shape
    hidden = d_act.shape[1]
    vmem = pl.BlockSpec(memory_space=pltpu.VMEM)
    return pl.pallas_call(
        functools.partial(latent_forward_kernel, group_rows, len(parts)),
        in_specs=[vmem] * (len(parts) + 4) + [ANY] * 4,
        out_specs=[vmem] * 10,
        out_shape=[
            shape_of((rows, width), BF16),
            shape_of((rows, LANES), F32),
            shape_of((rows, width), F32),
            shape_of((rows, width), BF16),
            shape_of((rows, 3 * width), BF16),
            shape_of((rows, width), BF16),
            shape_of((rows, width), F32),
            shape_of((rows, width), BF16),
            shape_of((rows, hidden), BF16),
            shape_of((rows, hidden), BF16),
        ],
        scratch_shapes=[pltpu.VMEM(w.shape, BF16) for w in weights]
        + [pltpu.SemaphoreType.DMA((4,))],
        compiler_params=params(),
        cost_estimate=cost(
            2 * rows * sum(w.size for w in weights),
            2 * sum(w.size for w in weights) + 4 * d_act.size,
            2 * d_act.size,
        ),
        name="latent_forward",
    )(*parts, latents, d_act, self_gain, mlp_gain, *weights)


def latent_backward_kernel(
    group_rows,
    d_hidden_ref,
    cot_ref,
    second_ref,
    first_ref,
    qkv_ref,
    cross_ref,
    stat_ref,
    self_gain_ref,
    mlp_gain_ref,
    w_in_hbm,
    w_self_hbm,
    w_qkv_hbm,
    w_cross_hbm,
    d_second_low_ref,
    d_qkv_ref,
    d_first_ref,
    d_first_low_ref,
    d_cross_ref,
    mlp_sum_ref,
    self_sum_ref,
    w_in,
    w_self,
    w_qkv,
    w_cross,
    d_inner,
    sems,
):
    loads = start_loads(
        (w_in_hbm, w_self_hbm, w_qkv_hbm, w_cross_hbm), (w_in, w_self, w_qkv, w_cross), sems
    )
    rows, width = cot_ref.shape
    scale = LANES**-0.5
    loads[0].wait()
    back, mlp_sum_ref[...] = norm_back(
        second_ref[...], mlp_gain_ref[...], dot(d_hidden_ref[...], w_in[...], NT)
    )
    d_second = cot_ref[...].astype(F32) + back
    d_first_ref[...] = d_second
    d_second_low_ref[...] = d_second.astype(BF16)
    loads[1].wait()
    d_inner[...] = dot(d_second_low_ref[...], w_self[...], NT).astype(BF16)
    for g in range(rows // group_rows):
        at = slice(g * group_rows, (g + 1) * group_rows)
        for h in range(HEADS):
            query = qkv_ref[at, head(h)]
            keys = qkv_ref[at, head(h, width)]
            grad = d_inner[at, head(h)]
            probs = self_softmax(query, keys)
            d_probs = dot(grad, qkv_ref[at, head(h, 2 * width)], NT)
            along = jnp.sum(probs * d_probs, axis=-1, keepdims=True)
            d_scores = (probs * (d_probs - along)).astype(BF16)
            d_qkv_ref[at, head(h)] = (dot(d_scores, keys) * scale).astype(BF16)
            d_qkv_ref[at, head(h, width)] = (dot(d_scores, query, TN) * scale).astype(BF16)
            d_qkv_ref[at, head(h, 2 * width)] = dot(probs.astype(BF16), grad, TN).astype(BF16)
    loads[2].wait()
    back, self_sum_ref[...] = norm_back(
        first_ref[...], self_gain_ref[...], dot(d_qkv_ref[...], w_qkv[...], NT)
    )
    d_first = d_first_ref[...] + back
    d_first_ref[...] = d_first
    d_first_low_ref[...] = d_first.astype(BF16)
    loads[3].wait()
    d_cross = dot(d_first_low_ref[...], w_cross[...], NT).astype(BF16)
    d_cross_ref[:, :width] = d_cross
    lane = lax.broadcasted_iota(jnp.int32, (rows, LANES), 1)
    delta = jnp.zeros((rows, LANES), F32)
    for h in range(HEADS):
        along = d_cross[:, head(h)].astype(F32) * cross_ref[:, head(h)].astype(F32)
        delta = jnp.where(lane == h, jnp.sum(along, axis=-1, keepdims=True), delta)
    packed = pack_stat(stat_ref[...]) + pltpu.roll(pack_stat(delta), 3 * HEADS, 1)
    d_cross_ref[:, width:] = packed.astype(BF16)


def latent_backward(group_rows, arrays, weights):
    d_hidden, cot = arrays[:2]
    rows, width = cot.shape
    vmem = pl.BlockSpec(memory_space=pltpu.VMEM)
    return pl.pallas_call(
        functools.partial(latent_backward_kernel, group_rows),
        in_specs=[vmem] * len(arrays) + [ANY] * 4,
        out_specs=[vmem] * 7,
        out_shape=[
            shape_of((rows, width), BF16),
            shape_of((rows, 3 * width), BF16),
            shape_of((rows, width), F32),
            shape_of((rows, width), BF16),
            shape_of((rows, width + LANES), BF16),
            shape_of((8, width), F32),
            shape_of((8, width), F32),
        ],
        scratch_shapes=[pltpu.VMEM(w.shape, BF16) for w in weights]
        + [pltpu.VMEM((rows, width), BF16), pltpu.SemaphoreType.DMA((4,))],
        compiler_params=params(),
        cost_estimate=cost(
            2 * rows * sum(w.size for w in weights), 2 * sum(w.size for w in weights)
        ),
        name="latent_backward",
    )(*arrays, *weights)


def reduced_weights(pairs, order):
    core = lax.rem(lax.axis_index("pix"), 2).astype(jnp.int32)
    sent = weight_half(pairs, jnp.reshape(1 - core, (1,)), None, order)
    kept = weight_half(pairs, jnp.reshape(core, (1,)), from_core(sent), order)
    total = reduce_parts(kept, order)
    begin, out = 0, []
    for _, right in pairs:
        width = right.shape[1] // lax.axis_size("pix")
        out.append(total[:, begin : begin + width])
        begin += width
    return out


def reduced_pix_weight(left, right, order):
    core = lax.rem(lax.axis_index("pix"), 2).astype(jnp.int32)
    sent = pix_weight_half(left, right, jnp.reshape(1 - core, (1,)), None, order)
    kept = pix_weight_half(left, right, jnp.reshape(core, (1,)), from_core(sent), order)
    return reduce_parts(kept, order)


def shards(
    latents,
    pixels,
    pixel_mask,
    cotangent,
    lat_gain,
    pix_gain,
    self_gain,
    mlp_gain,
    w_query,
    w_kv,
    w_cross_out,
    w_qkv,
    w_self_out,
    w_mlp_in,
    w_mlp_out,
):
    sizes = grid_sizes()
    own, group_rows, width = latents.shape
    groups, slots = pixel_mask.shape
    rows = own * group_rows
    lat_rows = latents.reshape(rows, width)
    cot_rows = cotangent.reshape(rows, width)
    pix_rows = pixels.reshape(groups * slots, width)
    gain_rows = [g.reshape(1, width) for g in (lat_gain, pix_gain, self_gain, mlp_gain)]
    lat_gain, pix_gain, self_gain, mlp_gain = gain_rows
    counts = jnp.sum(pixel_mask, axis=1, dtype=jnp.int32)

    here = lax.axis_index("pix")
    here_x, here_c = here // 2, lax.rem(here, 2)

    def groups_of(turn):
        holder_x = lax.rem(here_x + turn, sizes["x"])
        holders = [holder_x * 2 + here_c, holder_x * 2 + 1 - here_c]
        return [holder * own + i for holder in holders for i in range(own)]

    near = jnp.stack(groups_of(0)).astype(jnp.int32)
    turns = range(1, sizes["x"])
    far = [g for turn in turns for g in groups_of(turn)]
    far = jnp.stack(far).astype(jnp.int32) if far else None

    def spread(value):
        fars = []
        for turn in turns:
            moved = from_x(value, turn)
            fars += [moved, from_core(moved)]
        return jnp.concatenate([value, from_core(value)]), jnp.concatenate(fars)

    lat_low = norm_low(lat_rows.astype(F32), lat_gain)
    query = dot(lat_low, w_query).astype(BF16).reshape(own, group_rows, width)
    query_near, query_far = spread(query)
    pix_low, kv_rows = pix_project(pix_rows, pix_gain, w_kv)
    kv = kv_rows.reshape(groups, slots, 2 * width)

    mixed_far = cross_forward(far, counts, query_far, kv)
    mixed_far = mixed_far.reshape(sizes["x"] - 1, 2, own, group_rows, width + LANES)
    parts = []
    for turn in turns:
        joined = merge_call(mixed_far[turn - 1, 0], from_core(mixed_far[turn - 1, 1]))
        parts.append(from_x(joined, sizes["x"] - turn).reshape(rows, width + LANES))
    mixed_near = cross_forward(near, counts, query_near, kv)
    mixed_near = mixed_near.reshape(2, own, group_rows, width + LANES)
    joined = merge_call(mixed_near[0], from_core(mixed_near[1]))
    parts = [joined.reshape(rows, width + LANES)] + parts

    d_act = dot(cot_rows, w_mlp_out, NT)
    (
        cross_low,
        cross_stat,
        first,
        self_low,
        qkv,
        inner_low,
        second,
        mlp_low,
        act,
        d_hidden,
    ) = latent_forward(
        parts,
        group_rows,
        lat_rows,
        d_act,
        self_gain,
        mlp_gain,
        (w_cross_out, w_qkv, w_self_out, w_mlp_in),
    )
    latents_out = (second + dot(act, w_mlp_out)).astype(BF16)
    (sum_out,) = reduced_weights([(act, cot_rows)], "bxa")
    (sum_in,) = reduced_weights([(mlp_low, d_hidden)], "axb")
    d_second_low, d_qkv, d_first, d_first_low, d_cross, mlp_sum, self_sum = latent_backward(
        group_rows,
        (
            d_hidden,
            cot_rows,
            second,
            first,
            qkv,
            cross_low,
            cross_stat,
            self_gain,
            mlp_gain,
        ),
        (w_mlp_in, w_self_out, w_qkv, w_cross_out),
    )
    cross_near, cross_far = spread(d_cross.reshape(own, group_rows, width + LANES))
    sum_self, sum_qkv, sum_cross = reduced_weights(
        [(inner_low, d_second_low), (self_low, d_qkv), (cross_low, d_first_low)], "xba"
    )
    dq_near, d_kv = cross_backward(near, counts, query_near, cross_near, kv, None)
    dq_far, d_kv = cross_backward(far, counts, query_far, cross_far, kv, d_kv)
    dq_far = dq_far.reshape(sizes["x"] - 1, 2, own, group_rows, width)
    dq_near = dq_near.reshape(2, own, group_rows, width)
    terms = [dq_near[0], from_core(dq_near[1])]
    for turn in turns:
        joined = add_low(dq_far[turn - 1, 0], from_core(dq_far[turn - 1, 1]))
        terms.append(from_x(joined, sizes["x"] - turn))
    d_query = add_low(*terms).reshape(rows, width)
    d_kv_rows = d_kv.reshape(groups * slots, 2 * width)
    sum_kv = reduced_pix_weight(pix_low, d_kv_rows, "bxa")
    d_pixels, pix_sum = pix_back(d_kv_rows, w_kv, pix_rows, pix_gain)
    (sum_query,) = reduced_weights([(lat_low, d_query)], "xba")
    back, lat_sum = norm_back(lat_rows.astype(F32), lat_gain, dot(d_query, w_query, NT))
    d_latents = d_first + back
    gain_sums = jnp.stack([s.sum(0) for s in (lat_sum, pix_sum, self_sum, mlp_sum)])
    gain_sums = reduce_gains(gain_sums)
    return (
        latents_out.reshape(latents.shape),
        d_latents.reshape(latents.shape),
        d_pixels.reshape(pixels.shape),
        gain_sums[0],
        gain_sums[1],
        gain_sums[2],
        gain_sums[3],
        sum_query,
        sum_kv,
        sum_cross,
        sum_qkv,
        sum_self,
        sum_in,
        sum_out,
    )


def solution(mesh):
    held = P(("dp", "pix"), None, None)
    return jax.shard_map(
        shards,
        mesh=mesh,
        in_specs=(held, P("dp", "pix", None), P("dp", "pix"), held) + (P(),) * 11,
        out_specs=(held, held, P("dp", "pix", None)) + (P("dp"),) * 4 + (P("dp", "pix"),) * 7,
        check_vma=False,
    )
```

```python
import functools

import jax
import jax.numpy as jnp
from jax import lax
from jax.experimental import pallas as pl
from jax.experimental.pallas import tpu as pltpu
from jax.sharding import PartitionSpec as P

HEADS = 8
EPSILON = 1e-05
LANES = 128
EMPTY = -1e30
SCALE = LANES**-0.5
LOG2_E = 1.4426950408889634
F32 = jnp.float32
BF16 = jnp.bfloat16
NN = (((1,), (0,)), ((), ()))
NT = (((1,), (1,)), ((), ()))
TN = (((0,), (0,)), ((), ()))
ANY = pl.BlockSpec(memory_space=pl.ANY)
MIB = 1024 * 1024
FLOPS_PER_MICRO = 1.15e9


def bit_count(axis):
    size = lax.axis_size(axis)
    assert size & (size - 1) == 0
    return size.bit_length() - 1


CORE = ("pix", 0)


def orders():
    x = [("pix", i) for i in range(1, bit_count("pix"))]
    dp = [("dp", i) for i in range(bit_count("dp"))]
    fast, slow, rest = dp[:1], dp[1:2], dp[2:]
    return {
        "yxz": fast + x + slow + rest,
        "yzx": fast + slow + x + rest,
        "zyx": slow + fast + x + rest,
        "zxy": slow + x + fast + rest,
        "xyz": x + dp,
    }


def swap(value, bit):
    axis, place = bit
    pairs = [(p, p ^ (1 << place)) for p in range(lax.axis_size(axis))]
    return lax.ppermute(value, axis, pairs)


def add_low(*terms):
    total = terms[0].astype(F32)
    for term in terms[1:]:
        total = total + term.astype(F32)
    return total.astype(terms[0].dtype)


class Reduction:
    def __init__(self, kept, sent, order):
        self.steps = [(kept, sent)]
        for bit in order[:-1]:
            received = swap(sent, bit)
            kept, sent = add_low(kept[0], received[0]), add_low(kept[1], received[1])
            self.steps.append((kept, sent))
        self.total = kept.astype(F32) + swap(sent, order[-1]).astype(F32)


def step_of(reductions, step):
    return [array for reduction in reductions for array in reduction.steps[step]]


def behind(kernel, start, count):
    return lambda *refs: kernel(*refs[:start], *refs[start + count :])


def dot(left, right, dims=NN):
    return lax.dot_general(left, right, dims, preferred_element_type=F32)


def normalize(values):
    centred = values - jnp.mean(values, axis=-1, keepdims=True)
    root = lax.rsqrt(jnp.mean(centred * centred, axis=-1, keepdims=True) + EPSILON)
    return centred * root, root


def norm_low(values, gain):
    return (normalize(values)[0] * gain).astype(BF16)


def norm_back(values, gain, grad):
    hat, root = normalize(values)
    scaled = grad * gain
    along = jnp.mean(scaled * hat, axis=-1, keepdims=True)
    back = root * (scaled - jnp.mean(scaled, axis=-1, keepdims=True) - hat * along)
    parts = grad * hat
    return back, parts.reshape(parts.shape[0] // 8, 8, parts.shape[1]).sum(0)


def pack_stat(stat):
    lane = lax.broadcasted_iota(jnp.int32, stat.shape, 1)
    high = stat.astype(BF16).astype(F32)
    middle = (stat - high).astype(BF16).astype(F32)
    low = stat - high - middle
    packed = jnp.where(lane < HEADS, high, pltpu.roll(middle, HEADS, 1))
    packed = jnp.where(lane < 2 * HEADS, packed, pltpu.roll(low, 2 * HEADS, 1))
    return jnp.where(lane < 3 * HEADS, packed, 0.0)


def pack_rows(stats):
    pieces = []
    for stat in stats:
        high = stat.astype(BF16).astype(F32)
        middle = (stat - high).astype(BF16).astype(F32)
        pieces += [high, middle, stat - high - middle]
    empty = jnp.zeros((LANES - HEADS * len(pieces), pieces[0].shape[1]), F32)
    return jnp.concatenate(pieces + [empty], axis=0).T


def unpack_stat(packed):
    full = packed.astype(F32)
    return (
        full + pltpu.roll(full, LANES - HEADS, 1) + pltpu.roll(full, LANES - 2 * HEADS, 1)
    )


def head(index, base=0):
    return slice(base + index * LANES, base + (index + 1) * LANES)


def merge(first, second, width):
    first_stat = unpack_stat(first[:, width:])
    second_stat = unpack_stat(second[:, width:])
    top = jnp.maximum(first_stat, second_stat)
    first_weight = jnp.exp2(first_stat - top)
    second_weight = jnp.exp2(second_stat - top)
    total = first_weight + second_weight
    first_weight = first_weight / total
    second_weight = second_weight / total
    mixed = [
        first[:, head(h)].astype(F32) * first_weight[:, h : h + 1]
        + second[:, head(h)].astype(F32) * second_weight[:, h : h + 1]
        for h in range(HEADS)
    ]
    return mixed, top + jnp.log2(total)


def params(limit=56):
    return pltpu.CompilerParams(vmem_limit_bytes=limit * MIB)


def cost(micros):
    return pl.CostEstimate(
        flops=int(micros * FLOPS_PER_MICRO), bytes_accessed=0, transcendentals=0
    )


def shape_of(shape, dtype):
    return jax.ShapeDtypeStruct(shape, dtype)


def pix_project_kernel(pix_ref, gain_ref, weight_ref, low_ref, kv_ref):
    low = norm_low(pix_ref[...].astype(F32), gain_ref[...])
    low_ref[...] = low
    kv_ref[...] = dot(low, weight_ref[...]).astype(BF16)


def pix_project(pixels, gain, weight, after):
    rows, width = pixels.shape
    wide = weight.shape[1]
    block = 384 if rows % 384 == 0 else 128
    return pl.pallas_call(
        behind(pix_project_kernel, 3, len(after)),
        grid=(rows // block,),
        in_specs=[
            pl.BlockSpec((block, width), lambda i: (i, 0)),
            pl.BlockSpec((1, width), lambda i: (0, 0)),
            pl.BlockSpec((width, wide), lambda i: (0, 0)),
        ]
        + [ANY] * len(after),
        out_specs=[
            pl.BlockSpec((block, width), lambda i: (i, 0)),
            pl.BlockSpec((block, wide), lambda i: (i, 0)),
        ],
        out_shape=[shape_of((rows, width), BF16), shape_of((rows, wide), BF16)],
        compiler_params=params(),
        cost_estimate=cost(21),
        name="pix_project",
    )(pixels, gain, weight, *after)


def cross_forward_kernel(group_ref, count_ref, query_ref, kv_ref, out_ref):
    count = count_ref[group_ref[pl.program_id(0)]]
    width = query_ref.shape[2]
    slots = kv_ref.shape[1]
    valid = lax.broadcasted_iota(jnp.int32, (slots, 1), 0) < count
    ones = jnp.ones((slots, LANES), BF16)
    heads = range(HEADS)
    scores = [
        jnp.where(
            valid,
            dot(kv_ref[0, :, head(h)], query_ref[0, :, head(h)], NT) * (SCALE * LOG2_E),
            EMPTY,
        )
        for h in heads
    ]
    tops = [jnp.max(s, axis=0, keepdims=True) for s in scores]
    expos = [jnp.exp2(s - t) for s, t in zip(scores, tops)]
    totals = [jnp.sum(e, axis=0, keepdims=True) for e in expos]
    expos = [e.astype(BF16) for e in expos]
    for h in heads:
        values = jnp.concatenate([kv_ref[0, :, head(h, width)], ones], axis=1)
        mixed = dot(expos[h], values, TN)
        out_ref[0, :, head(h)] = (mixed[:, :LANES] * (1.0 / mixed[:, LANES:])).astype(BF16)
    stat = jnp.concatenate(tops, axis=0) + jnp.log2(jnp.concatenate(totals, axis=0))
    out_ref[0, :, width:] = pack_rows([stat]).astype(BF16)


def cross_forward(groups, counts, query, kv, after):
    number, rows, width = query.shape
    slots, wide = kv.shape[1:]
    return pl.pallas_call(
        behind(cross_forward_kernel, 4, len(after)),
        grid_spec=pltpu.PrefetchScalarGridSpec(
            num_scalar_prefetch=2,
            grid=(number,),
            in_specs=[
                pl.BlockSpec((1, rows, width), lambda i, g, n: (i, 0, 0)),
                pl.BlockSpec((1, slots, wide), lambda i, g, n: (g[i], 0, 0)),
            ]
            + [ANY] * len(after),
            out_specs=pl.BlockSpec((1, rows, width + LANES), lambda i, g, n: (i, 0, 0)),
        ),
        out_shape=shape_of((number, rows, width + LANES), BF16),
        compiler_params=params(),
        cost_estimate=cost(5),
        name="cross_forward",
    )(groups, counts, query, kv, *after)


def merge_kernel(first_ref, second_ref, out_ref):
    width = out_ref.shape[2] - LANES
    mixed, stat = merge(first_ref[0], second_ref[0], width)
    for h in range(HEADS):
        out_ref[0, :, head(h)] = mixed[h].astype(BF16)
    out_ref[0, :, width:] = pack_stat(stat).astype(BF16)


def merge_call(first, second):
    number, rows, wide = first.shape
    spec = pl.BlockSpec((1, rows, wide), lambda i: (i, 0, 0))
    return pl.pallas_call(
        merge_kernel,
        grid=(number,),
        in_specs=[spec, spec],
        out_specs=spec,
        out_shape=shape_of(first.shape, BF16),
        compiler_params=params(),
        cost_estimate=cost(3),
        name="merge",
    )(first, second)


def cross_backward_kernel(group_ref, count_ref, query_ref, grad_ref, kv_ref, dq_ref, dkv_ref):
    count = count_ref[group_ref[pl.program_id(0)]]
    width = query_ref.shape[2]
    slots = kv_ref.shape[1]
    valid = lax.broadcasted_iota(jnp.int32, (slots, 1), 0) < count
    stat = grad_ref[0, :, width:].astype(F32).T
    pieces = [stat[HEADS * i : HEADS * (i + 1)] for i in range(6)]
    log_total = pieces[0] + pieces[1] + pieces[2]
    delta = pieces[3] + pieces[4] + pieces[5]
    heads = range(HEADS)
    scores = [
        dot(kv_ref[0, :, head(h)], query_ref[0, :, head(h)], NT) * (SCALE * LOG2_E)
        - log_total[h : h + 1]
        for h in heads
    ]
    probs = [jnp.where(valid, jnp.exp2(s), 0.0) for s in scores]
    d_probs = [dot(kv_ref[0, :, head(h, width)], grad_ref[0, :, head(h)], NT) for h in heads]
    d_scores = [(probs[h] * (d_probs[h] - delta[h : h + 1])).astype(BF16) for h in heads]
    probs = [p.astype(BF16) for p in probs]
    for h in heads:
        dkv_ref[0, :, head(h)] = (dot(d_scores[h], query_ref[0, :, head(h)]) * SCALE).astype(BF16)
        dkv_ref[0, :, head(h, width)] = dot(probs[h], grad_ref[0, :, head(h)]).astype(BF16)
        dq_ref[0, :, head(h)] = (dot(d_scores[h], kv_ref[0, :, head(h)], TN) * SCALE).astype(BF16)


def cross_backward(groups, counts, query, grad, kv, old, after):
    number, rows, width = query.shape
    slots, wide = kv.shape[1:]
    olds = [] if old is None else [old]
    extra = olds + list(after)
    return pl.pallas_call(
        behind(cross_backward_kernel, 5, len(extra)),
        grid_spec=pltpu.PrefetchScalarGridSpec(
            num_scalar_prefetch=2,
            grid=(number,),
            in_specs=[
                pl.BlockSpec((1, rows, width), lambda i, g, n: (i, 0, 0)),
                pl.BlockSpec((1, rows, width + LANES), lambda i, g, n: (i, 0, 0)),
                pl.BlockSpec((1, slots, wide), lambda i, g, n: (g[i], 0, 0)),
            ]
            + [ANY] * len(extra),
            out_specs=[
                pl.BlockSpec((1, rows, width), lambda i, g, n: (i, 0, 0)),
                pl.BlockSpec((1, slots, wide), lambda i, g, n: (g[i], 0, 0)),
            ],
        ),
        out_shape=[shape_of((number, rows, width), BF16), shape_of(kv.shape, BF16)],
        input_output_aliases={} if old is None else {5: 1},
        compiler_params=params(),
        cost_estimate=cost(6.5),
        name="cross_backward",
    )(groups, counts, query, grad, kv, *extra)


def pix_back_kernel(dkv_ref, weight_ref, pix_ref, gain_ref, out_ref):
    back, _ = norm_back(
        pix_ref[...].astype(F32), gain_ref[...], dot(dkv_ref[...], weight_ref[...], NT)
    )
    out_ref[...] = back.astype(BF16)


def pix_back(dkv, weight, pixels, gain, after):
    rows, width = pixels.shape
    wide = weight.shape[1]
    block = 384 if rows % 384 == 0 else 128
    return pl.pallas_call(
        behind(pix_back_kernel, 4, len(after)),
        grid=(rows // block,),
        in_specs=[
            pl.BlockSpec((block, wide), lambda i: (i, 0)),
            pl.BlockSpec((width, wide), lambda i: (0, 0)),
            pl.BlockSpec((block, width), lambda i: (i, 0)),
            pl.BlockSpec((1, width), lambda i: (0, 0)),
        ]
        + [ANY] * len(after),
        out_specs=pl.BlockSpec((block, width), lambda i: (i, 0)),
        out_shape=shape_of((rows, width), BF16),
        compiler_params=params(),
        cost_estimate=cost(22),
        name="pix_back",
    )(dkv, weight, pixels, gain, *after)


def places(order, second):
    found = []
    rest = order[2:]
    for code in range(2 ** (len(order) - 1)):
        first, spot = code & 1, tuple((code >> (1 + k)) & 1 for k in range(len(rest)))
        offset = {"dp": 0, "pix": 0}
        for bit, on in [(order[0], first)] + list(zip(rest, spot)):
            offset[bit[0]] += on << bit[1]
        found.append((first, spot, offset["dp"], offset["pix"]))
    axis, place = order[1]
    moving = second << place
    found.sort(key=lambda entry: (entry[2], entry[3]))
    return found, (moving if axis == "dp" else 0), (moving if axis == "pix" else 0)


def weight_kernel(order, devices, columns, number, sides, here_ref, *refs):
    inputs = 2 * number * sides
    operands, added, outs, scratch = refs[:inputs], refs[inputs:-3], refs[-3:-1], refs[-1]
    found, step_dp, step_pix = places(order, pl.program_id(0))
    for first, spot, dp, pix in found:
        own = here_ref[0] ^ (dp + step_dp)
        block = here_ref[1] ^ (pix + step_pix)
        begin = 0
        for k in range(number):
            tall = operands[2 * k * sides].shape[1] // devices
            width = operands[2 * k * sides + 1].shape[1] // columns
            whole = tall % LANES == 0
            at_rows = own * tall if whole else own * tall // LANES * LANES
            at_rows = pl.ds(pl.multiple_of(at_rows, LANES), max(tall, LANES))
            at_columns = pl.ds(pl.multiple_of(block * width, LANES), width)
            part = None
            for side in range(sides):
                left, right = operands[2 * (k * sides + side) : 2 * (k * sides + side) + 2]
                term = dot(left[:, at_rows], right[:, at_columns], TN)
                part = term if part is None else part + term
            if not whole:
                scratch[:, :width] = part
                inside = pl.multiple_of(lax.rem(own * tall, LANES), tall)
                part = scratch[pl.ds(inside, tall), :width]
            at = (0,) + spot + (slice(None), slice(begin, begin + width))
            outs[first][at] = part.astype(BF16)
            begin += width
        for extra in added:
            tall = extra.shape[0] // devices
            at = (0,) + spot + (slice(None), slice(begin, begin + extra.shape[1]))
            rows = pl.ds(pl.multiple_of(own * tall, tall), tall)
            outs[first][at] = extra[rows, :].astype(BF16)
            begin += extra.shape[1]


def weight_blocks(pairs, added, here, order, after):
    devices = lax.axis_size("dp")
    columns = lax.axis_size("pix")
    depth = pairs[0][0][0][0].shape[0]
    sides = len(pairs[0][0][0])
    rows = pairs[0][0][1] // devices
    width = sum(right[1] for _, right in pairs) // columns + sum(a.shape[1] for a in added)
    bits = len(order) - 1
    full = (2,) * bits + (rows, width)
    out_spec = pl.BlockSpec((1,) + full[1:], lambda i, h: (i,) + (0,) * (bits + 1))
    arrays, specs = [], []
    for pair in pairs:
        for side in range(sides):
            for group, wide, index in pair:
                arrays.append(group[side])
                specs.append(pl.BlockSpec((depth, wide), lambda i, h, index=index: (0, index)))
    specs += [pl.BlockSpec(array.shape, lambda i, h: (0, 0)) for array in added]
    inputs = arrays + list(added)
    kernel = functools.partial(weight_kernel, order, devices, columns, len(pairs), sides)
    return pl.pallas_call(
        behind(kernel, 1 + len(inputs), len(after)),
        grid_spec=pltpu.PrefetchScalarGridSpec(
            num_scalar_prefetch=1,
            grid=(2,),
            in_specs=specs + [ANY] * len(after),
            out_specs=[out_spec, out_spec],
            scratch_shapes=[pltpu.VMEM((LANES, width), F32)],
        ),
        out_shape=[shape_of(full, BF16)] * 2,
        compiler_params=params(),
        cost_estimate=cost(6.5),
        name="weight_blocks",
    )(here, *inputs, *after)


def pix_weight_kernel(splits, devices, columns, here_ref, left_ref, right_ref, weight_ref, *refs):
    outs, sum_ref, total_ref = refs[:-2], refs[-2], refs[-1]
    step = pl.program_id(0)
    left = left_ref[...]
    wide = total_ref.shape[2]

    def add(first):
        for p in range(columns):
            grad = dot(left, right_ref[:, p * wide : (p + 1) * wide], TN)
            total_ref[p] = grad if first else total_ref[p] + grad

    pl.when(step == 0)(lambda: add(True))
    pl.when(step > 0)(lambda: add(False))

    @pl.when(step == pl.num_programs(0) - 1)
    def _():
        height = left_ref.shape[1] // devices
        width = wide // len(splits)
        sums = jnp.zeros(sum_ref.shape, F32)
        for p in range(columns):
            for h in range(wide // LANES):
                weight = weight_ref[:, head(h, p * wide)].astype(F32)
                sums = sums + total_ref[p, :, head(h)] * weight
        sum_ref[...] = sums
        for k, order in enumerate(splits):
            for second in range(2):
                found, step_dp, step_pix = places(order, second)
                for first, spot, dp, pix in found:
                    own = here_ref[0] ^ (dp + step_dp)
                    block = here_ref[1] ^ (pix + step_pix)
                    at_rows = pl.ds(pl.multiple_of(own * height, 32), height)
                    part = total_ref[block, at_rows, k * width : (k + 1) * width]
                    outs[2 * k + first][(second,) + spot] = part.astype(BF16)


def pix_weight(left, right, weight, here, splits, after):
    depth, height = left.shape
    devices = lax.axis_size("dp")
    columns = lax.axis_size("pix")
    wide = right.shape[1]
    width = wide // columns
    bits = len(splits[0]) - 1
    full = (2,) * bits + (height // devices, width // len(splits))
    block = 768 if depth % 768 == 0 else 128
    whole = pl.BlockSpec(full, lambda i, h: (0,) * len(full))
    kernel = functools.partial(pix_weight_kernel, splits, devices, columns)
    return pl.pallas_call(
        behind(kernel, 4, len(after)),
        grid_spec=pltpu.PrefetchScalarGridSpec(
            num_scalar_prefetch=1,
            grid=(depth // block,),
            in_specs=[
                pl.BlockSpec((block, height), lambda i, h: (i, 0)),
                pl.BlockSpec((block, wide), lambda i, h: (i, 0)),
                pl.BlockSpec((height, wide), lambda i, h: (0, 0)),
            ]
            + [ANY] * len(after),
            out_specs=[whole] * (2 * len(splits)) + [pl.BlockSpec((height, LANES), lambda i, h: (0, 0))],
            scratch_shapes=[pltpu.VMEM((columns, height, width), F32)],
        ),
        out_shape=[shape_of(full, BF16)] * (2 * len(splits)) + [shape_of((height, LANES), F32)],
        compiler_params=params(),
        cost_estimate=cost(23),
        name="pix_weight",
    )(here, left, right, weight, *after)


def query_kernel(lat_ref, gain_ref, weight_ref, low_ref, query_ref):
    low = norm_low(lat_ref[...].astype(F32), gain_ref[...])
    low_ref[...] = low
    query_ref[...] = dot(low, weight_ref[...]).astype(BF16)


def query_project(latents, gain, weight):
    rows, width = latents.shape
    return pl.pallas_call(
        query_kernel,
        out_shape=[shape_of((rows, width), BF16)] * 2,
        compiler_params=params(),
        cost_estimate=cost(3.5),
        name="query_project",
    )(latents, gain, weight)


def latent_end_kernel(count, *refs):
    terms = refs[:count]
    lat_ref, gain_ref, weight_ref, d_first_ref, query_ref, out_ref, sum_ref = refs[count:]
    total = terms[0][...].astype(F32)
    for term in terms[1:]:
        total = total + term[...].astype(F32)
    low = total.astype(BF16)
    query_ref[...] = low
    back, sum_ref[...] = norm_back(
        lat_ref[...].astype(F32), gain_ref[...], dot(low, weight_ref[...], NT)
    )
    out_ref[...] = d_first_ref[...] + back


def latent_end(terms, latents, gain, weight, d_first, after):
    rows, width = latents.shape
    vmem = pl.BlockSpec(memory_space=pltpu.VMEM)
    return pl.pallas_call(
        behind(functools.partial(latent_end_kernel, len(terms)), len(terms) + 4, len(after)),
        in_specs=[vmem] * (len(terms) + 4) + [ANY] * len(after),
        out_specs=[vmem] * 3,
        out_shape=[
            shape_of((rows, width), BF16),
            shape_of((rows, width), F32),
            shape_of((8, width), F32),
        ],
        compiler_params=params(),
        cost_estimate=cost(4.7),
        name="latent_end",
    )(*terms, latents, gain, weight, d_first, *after)


def start_loads(sources, targets, sems):
    copies = [
        pltpu.make_async_copy(source, target, sems.at[i])
        for i, (source, target) in enumerate(zip(sources, targets))
    ]
    for copy in copies:
        copy.start()
    return copies


def self_softmax(query, keys):
    scores = dot(keys, query, NT) * (SCALE * LOG2_E)
    expo = jnp.exp2(scores - jnp.max(scores, axis=0, keepdims=True))
    return expo * (1.0 / jnp.sum(expo, axis=0, keepdims=True))


def latent_forward_kernel(
    group_rows,
    part_count,
    *refs,
):
    parts = refs[:part_count]
    (
        lat_ref,
        cot_ref,
        self_gain_ref,
        mlp_gain_ref,
        w_cross_hbm,
        w_qkv_hbm,
        w_self_hbm,
        w_in_hbm,
        w_out_hbm,
        acts_ref,
        lows_ref,
        stat_ref,
        first_ref,
        qkv_ref,
        second_ref,
        out_ref,
        w_cross,
        w_qkv,
        w_self,
        w_in,
        w_out,
        hidden_ref,
        d_act_ref,
        sems,
    ) = refs[part_count:]
    loads = start_loads(
        (w_cross_hbm, w_qkv_hbm, w_self_hbm, w_in_hbm, w_out_hbm),
        (w_cross, w_qkv, w_self, w_in, w_out),
        sems,
    )
    rows, width = lat_ref.shape
    mlp_low_ref, self_low_ref, inner_ref, cross_ref = (
        lows_ref.at[:, i * width : (i + 1) * width] for i in range(4)
    )
    act_ref, d_hidden_ref = (
        acts_ref.at[:, i * w_in.shape[1] : (i + 1) * w_in.shape[1]] for i in range(2)
    )
    joined = parts[0][...]
    for i, part in enumerate(parts[1:]):
        mixed, stat = merge(joined, part[...], width)
        if i < part_count - 2:
            joined = jnp.concatenate(
                [m.astype(BF16) for m in mixed] + [pack_stat(stat).astype(BF16)], axis=1
            )
    for h in range(HEADS):
        cross_ref[:, head(h)] = mixed[h].astype(BF16)
    stat_ref[...] = stat
    loads[0].wait()
    first = lat_ref[...].astype(F32) + dot(cross_ref[...], w_cross[...])
    first_ref[...] = first
    self_low_ref[...] = norm_low(first, self_gain_ref[...])
    loads[1].wait()
    for part in range(3):
        cols = slice(part * width, (part + 1) * width)
        qkv_ref[:, cols] = dot(self_low_ref[...], w_qkv[:, cols]).astype(BF16)
    spots = [
        (slice(g * group_rows, (g + 1) * group_rows), h)
        for g in range(rows // group_rows)
        for h in range(HEADS)
    ]
    probs = [
        self_softmax(qkv_ref[at, head(h)], qkv_ref[at, head(h, width)]).astype(BF16)
        for at, h in spots
    ]
    for (at, h), p in zip(spots, probs):
        inner_ref[at, head(h)] = dot(p, qkv_ref[at, head(h, 2 * width)], TN).astype(BF16)
    loads[2].wait()
    second = first_ref[...] + dot(inner_ref[...], w_self[...])
    second_ref[...] = second
    mlp_low_ref[...] = norm_low(second, mlp_gain_ref[...])
    loads[3].wait()
    loads[4].wait()
    chunk = hidden_ref.shape[2]
    chunks = w_in.shape[1] // chunk

    def multiply(i, slot):
        at = pl.ds(pl.multiple_of(i * chunk, chunk), chunk)
        hidden_ref[slot] = dot(mlp_low_ref[...], w_in[:, at])
        d_act_ref[slot] = dot(cot_ref[...], w_out[at, :], NT)

    def activate(i, slot):
        at = pl.ds(pl.multiple_of(i * chunk, chunk), chunk)
        hidden = hidden_ref[slot]
        gate = 0.5 + 0.5 * lax.erf(hidden * 0.5**0.5)
        bell = jnp.exp2((-0.5 * LOG2_E) * hidden * hidden) * 0.3989422804014327
        act_ref[:, at] = (hidden * gate).astype(BF16)
        d_hidden_ref[:, at] = (d_act_ref[slot] * (gate + hidden * bell)).astype(BF16)

    multiply(0, 0)

    def step(i, carry):
        slot = lax.rem(i, 2)
        multiply(i + 1, 1 - slot)
        activate(i, slot)
        return carry

    lax.fori_loop(0, chunks - 1, step, 0)
    activate(chunks - 1, (chunks - 1) % 2)
    out_ref[...] = (second_ref[...] + dot(act_ref[...], w_out[...])).astype(BF16)


def latent_forward(parts, group_rows, latents, cot, self_gain, mlp_gain, weights, after):
    rows, width = latents.shape
    hidden = weights[3].shape[1]
    vmem = pl.BlockSpec(memory_space=pltpu.VMEM)
    return pl.pallas_call(
        behind(
            functools.partial(latent_forward_kernel, group_rows, len(parts)),
            len(parts) + 9,
            len(after),
        ),
        in_specs=[vmem] * (len(parts) + 4) + [ANY] * (5 + len(after)),
        out_specs=[vmem] * 7,
        out_shape=[
            shape_of((rows, 2 * hidden), BF16),
            shape_of((rows, 4 * width), BF16),
            shape_of((rows, LANES), F32),
            shape_of((rows, width), F32),
            shape_of((rows, 3 * width), BF16),
            shape_of((rows, width), F32),
            shape_of((rows, width), BF16),
        ],
        scratch_shapes=[pltpu.VMEM(w.shape, BF16) for w in weights]
        + [pltpu.VMEM((2, rows, 512), F32)] * 2
        + [pltpu.SemaphoreType.DMA((5,))],
        compiler_params=params(),
        cost_estimate=cost(20),
        name="latent_forward",
    )(*parts, latents, cot, self_gain, mlp_gain, *weights, *after)


def latent_backward_kernel(
    group_rows,
    acts_hbm,
    lows_hbm,
    cot_ref,
    second_ref,
    first_ref,
    qkv_ref,
    stat_ref,
    self_gain_ref,
    mlp_gain_ref,
    w_in_hbm,
    w_self_hbm,
    w_qkv_hbm,
    w_cross_hbm,
    grads_ref,
    d_first_ref,
    d_cross_ref,
    mlp_sum_ref,
    self_sum_ref,
    w_in,
    w_self,
    w_qkv,
    w_cross,
    d_inner,
    d_hidden_ref,
    cross_ref,
    sems,
):
    rows, width = cot_ref.shape
    hidden = d_hidden_ref.shape[1]
    loads = start_loads(
        (
            acts_hbm.at[:, hidden : 2 * hidden],
            w_in_hbm,
            w_self_hbm,
            w_qkv_hbm,
            w_cross_hbm,
            lows_hbm.at[:, 3 * width : 4 * width],
        ),
        (d_hidden_ref, w_in, w_self, w_qkv, w_cross, cross_ref),
        sems,
    )
    d_qkv_ref = grads_ref.at[:, : 3 * width]
    d_second_low_ref = grads_ref.at[:, 3 * width : 4 * width]
    d_first_low_ref = grads_ref.at[:, 4 * width :]
    loads[0].wait()
    loads[1].wait()
    back, mlp_sum_ref[...] = norm_back(
        second_ref[...], mlp_gain_ref[...], dot(d_hidden_ref[...], w_in[...], NT)
    )
    d_second = cot_ref[...].astype(F32) + back
    d_first_ref[...] = d_second
    d_second_low_ref[...] = d_second.astype(BF16)
    loads[2].wait()
    d_inner[...] = dot(d_second_low_ref[...], w_self[...], NT).astype(BF16)
    for g in range(rows // group_rows):
        at = slice(g * group_rows, (g + 1) * group_rows)
        heads = range(HEADS)
        probs = [self_softmax(qkv_ref[at, head(h)], qkv_ref[at, head(h, width)]) for h in heads]
        d_probs = [dot(qkv_ref[at, head(h, 2 * width)], d_inner[at, head(h)], NT) for h in heads]
        alongs = [jnp.sum(p * d, axis=0, keepdims=True) for p, d in zip(probs, d_probs)]
        d_scores = [(p * (d - a)).astype(BF16) for p, d, a in zip(probs, d_probs, alongs)]
        for h in heads:
            query = qkv_ref[at, head(h)]
            keys = qkv_ref[at, head(h, width)]
            d_qkv_ref[at, head(h)] = (dot(d_scores[h], keys, TN) * SCALE).astype(BF16)
            d_qkv_ref[at, head(h, width)] = (dot(d_scores[h], query) * SCALE).astype(BF16)
            d_qkv_ref[at, head(h, 2 * width)] = dot(
                probs[h].astype(BF16), d_inner[at, head(h)]
            ).astype(BF16)
    loads[3].wait()
    back, self_sum_ref[...] = norm_back(
        first_ref[...], self_gain_ref[...], dot(d_qkv_ref[...], w_qkv[...], NT)
    )
    d_first = d_first_ref[...] + back
    d_first_ref[...] = d_first
    d_first_low_ref[...] = d_first.astype(BF16)
    loads[4].wait()
    loads[5].wait()
    d_cross = dot(d_first_low_ref[...], w_cross[...], NT).astype(BF16)
    d_cross_ref[:, :width] = d_cross
    lane = lax.broadcasted_iota(jnp.int32, (rows, LANES), 1)
    delta = jnp.zeros((rows, LANES), F32)
    for h in range(HEADS):
        along = d_cross[:, head(h)].astype(F32) * cross_ref[:, head(h)].astype(F32)
        delta = jnp.where(lane == h, jnp.sum(along, axis=-1, keepdims=True), delta)
    packed = pack_stat(stat_ref[...]) + pltpu.roll(pack_stat(delta), 3 * HEADS, 1)
    d_cross_ref[:, width:] = packed.astype(BF16)


def latent_backward(group_rows, acts, lows, arrays, weights, after):
    rows, width = arrays[0].shape
    vmem = pl.BlockSpec(memory_space=pltpu.VMEM)
    return pl.pallas_call(
        behind(
            functools.partial(latent_backward_kernel, group_rows), len(arrays) + 6, len(after)
        ),
        in_specs=[ANY, ANY] + [vmem] * len(arrays) + [ANY] * (4 + len(after)),
        out_specs=[vmem] * 5,
        out_shape=[
            shape_of((rows, 5 * width), BF16),
            shape_of((rows, width), F32),
            shape_of((rows, width + LANES), BF16),
            shape_of((8, width), F32),
            shape_of((8, width), F32),
        ],
        scratch_shapes=[pltpu.VMEM(w.shape, BF16) for w in weights]
        + [
            pltpu.VMEM((rows, width), BF16),
            pltpu.VMEM((rows, acts.shape[1] // 2), BF16),
            pltpu.VMEM((rows, width), BF16),
            pltpu.SemaphoreType.DMA((6,)),
        ],
        compiler_params=params(),
        cost_estimate=cost(15.5),
        name="latent_backward",
    )(acts, lows, *arrays, *weights, *after)


def shards(
    latents,
    pixels,
    pixel_mask,
    cotangent,
    lat_gain,
    pix_gain,
    self_gain,
    mlp_gain,
    w_query,
    w_kv,
    w_cross_out,
    w_qkv,
    w_self_out,
    w_mlp_in,
    w_mlp_out,
):
    own, group_rows, width = latents.shape
    groups, slots = pixel_mask.shape
    rows = own * group_rows
    lat_rows = latents.reshape(rows, width)
    cot_rows = cotangent.reshape(rows, width)
    pix_rows = pixels.reshape(groups * slots, width)
    gain_rows = [g.reshape(1, width) for g in (lat_gain, pix_gain, self_gain, mlp_gain)]
    lat_gain, pix_gain, self_gain, mlp_gain = gain_rows
    counts = jnp.sum(pixel_mask, axis=1, dtype=jnp.int32)
    order = orders()
    pix_here = lax.axis_index("pix").astype(jnp.int32)
    dp_here = lax.axis_index("dp").astype(jnp.int32)
    here = jnp.stack([dp_here, pix_here])

    holders = lax.axis_size("pix")
    of_holder = [
        jnp.stack([(pix_here ^ r) * own + i for i in range(own)]).astype(jnp.int32)
        for r in range(holders)
    ]
    ranked = list(range(2, holders)) + [1, 0]

    def hop(value, distance):
        pairs = [(p, p ^ distance) for p in range(holders)]
        return value if distance == 0 else lax.ppermute(value, "pix", pairs)

    lat_low, query = query_project(lat_rows, lat_gain, w_query)
    query = query.reshape(own, group_rows, width)
    queries = [hop(query, r - r % 2) for r in range(holders)]
    queries = [swap(q, CORE) if r % 2 else q for r, q in enumerate(queries)]
    pix_low, kv_rows = pix_project(pix_rows, pix_gain, w_kv, [query])
    kv = kv_rows.reshape(groups, slots, 2 * width)

    mixed = {}
    last = []
    for r in ranked:
        if r == 1:
            joined = {
                far: merge_call(mixed[far], swap(mixed[far + 1], CORE))
                for far in range(2, holders, 2)
            }
            last = list(joined.values())
        mixed[r] = cross_forward(of_holder[r], counts, queries[r], kv, last)
        last = [mixed[r]]
    parts = [mixed[0], swap(mixed[1], CORE)] + [hop(joined[far], far) for far in joined]
    parts = [part.reshape(rows, width + LANES) for part in parts]

    acts, lows, cross_stat, first, qkv, second, latents_out = latent_forward(
        parts,
        group_rows,
        lat_rows,
        cot_rows,
        self_gain,
        mlp_gain,
        (w_cross_out, w_qkv, w_self_out, w_mlp_in, w_mlp_out),
        [],
    )
    grads_low, d_first, d_cross, mlp_sum, self_sum = latent_backward(
        group_rows,
        acts,
        lows,
        (cot_rows, second, first, qkv, cross_stat, self_gain, mlp_gain),
        (w_mlp_in, w_self_out, w_qkv, w_cross_out),
        [],
    )
    d_cross = d_cross.reshape(own, group_rows, width + LANES)
    grads = {0: d_cross, 1: swap(d_cross, CORE)}
    for far in range(2, holders, 2):
        grads[far] = hop(d_cross, far)
        grads[far + 1] = swap(grads[far], CORE)

    both_cot = (cot_rows, swap(cot_rows, CORE))
    both_acts = (acts, swap(acts, CORE))
    both_lows = (lows, swap(lows, CORE))
    both_grads = (grads_low, swap(grads_low, CORE))
    wide = acts.shape[1] // 2
    out_parts = weight_blocks(
        [((both_acts, wide, 0), (both_cot, width, 0))], [], here, order["yzx"], [grads_low]
    )
    out_sum = Reduction(*out_parts, order["yzx"])
    in_parts = weight_blocks(
        [((both_lows, width, 0), (both_acts, wide, 1))], [], here, order["zyx"], out_parts
    )
    in_sum = Reduction(*in_parts, order["zyx"])
    self_pairs = [
        ((both_lows, width, 2), (both_grads, width, 3)),
        ((both_lows, width, 1), (both_grads, 3 * width, 0)),
        ((both_lows, width, 3), (both_grads, width, 4)),
    ]
    self_parts = weight_blocks(self_pairs, [], here, order["xyz"], in_parts)
    self_total = Reduction(*self_parts, order["xyz"])
    dqs = {}
    dqs[0], d_kv = cross_backward(of_holder[0], counts, queries[0], grads[0], kv, None, self_parts)
    dqs[1], d_kv = cross_backward(of_holder[1], counts, queries[1], grads[1], kv, d_kv, [])
    last = []
    for r in range(2, holders):
        dqs[r], d_kv = cross_backward(of_holder[r], counts, queries[r], grads[r], kv, d_kv, last)
        last = []
    terms = [dqs[0], swap(dqs[1], CORE)]
    for far in range(2, holders, 2):
        terms.append(hop(add_low(dqs[far], swap(dqs[far + 1], CORE)), far))
    terms = [term.reshape(rows, width) for term in terms]
    d_kv_rows = d_kv.reshape(groups * slots, 2 * width)
    splits = [[CORE] + order[name] for name in ("yzx", "zyx")]
    *kv_parts, kv_rows_sum = pix_weight(
        pix_low, d_kv_rows, w_kv, here, splits, step_of((out_sum, in_sum), 1)
    )
    kv_sums = [Reduction(*kv_parts[2 * k : 2 * k + 2], splits[k]) for k in range(2)]
    d_query, d_latents, lat_sum = latent_end(
        terms,
        lat_rows,
        lat_gain,
        w_query,
        d_first,
        [kv_rows_sum] + step_of((self_total,), 1),
    )
    gains = jnp.stack(
        [lat_sum.sum(0), kv_rows_sum.sum(1) / pix_gain[0], self_sum.sum(0), mlp_sum.sum(0)], axis=1
    )
    gains = jnp.pad(gains, ((0, 0), (0, LANES - gains.shape[1])))
    query_order = [CORE] + order["xyz"]
    query_pairs = [(((lat_low,), width, 0), ((d_query,), width, 0))]
    query_parts = weight_blocks(query_pairs, [gains], here, query_order, [])
    query_sum = Reduction(*query_parts, query_order)
    d_pixels = pix_back(
        d_kv_rows, w_kv, pix_rows, pix_gain, list(query_parts) + step_of(kv_sums, 1)
    )
    split_at = width // holders
    sums = query_sum.total
    return (
        latents_out.reshape(latents.shape),
        d_latents.reshape(latents.shape),
        d_pixels.reshape(pixels.shape),
        sums[:, split_at],
        sums[:, split_at + 1],
        sums[:, split_at + 2],
        sums[:, split_at + 3],
        sums[:, :split_at],
        jnp.concatenate([half.total for half in kv_sums], axis=1),
        self_total.total[:, 4 * split_at :],
        self_total.total[:, split_at : 4 * split_at],
        self_total.total[:, :split_at],
        in_sum.total,
        out_sum.total,
    )


def solution(mesh):
    held = P(("dp", "pix"), None, None)
    return jax.shard_map(
        shards,
        mesh=mesh,
        in_specs=(held, P("dp", "pix", None), P("dp", "pix"), held) + (P(),) * 11,
        out_specs=(held, held, P("dp", "pix", None)) + (P("dp"),) * 4 + (P("dp", "pix"),) * 7,
        check_vma=False,
    )
```

```python
import functools

import jax
import jax.numpy as jnp
from jax import lax
from jax.experimental import pallas as pl
from jax.experimental.pallas import tpu as pltpu
from jax.sharding import PartitionSpec as P

HEADS = 8
EPSILON = 1e-05
LANES = 128
EMPTY = -1e30
SCALE = LANES**-0.5
LOG2_E = 1.4426950408889634
F32 = jnp.float32
BF16 = jnp.bfloat16
NN = (((1,), (0,)), ((), ()))
NT = (((1,), (1,)), ((), ()))
TN = (((0,), (0,)), ((), ()))
ANY = pl.BlockSpec(memory_space=pl.ANY)
MIB = 1024 * 1024
FLOPS_PER_MICRO = 0.5e9


def bit_count(axis):
    size = lax.axis_size(axis)
    assert size & (size - 1) == 0
    return size.bit_length() - 1


CORE = ("pix", 0)


def orders():
    x = [("pix", i) for i in range(1, bit_count("pix"))]
    dp = [("dp", i) for i in range(bit_count("dp"))]
    fast, slow, rest = dp[:1], dp[1:2], dp[2:]
    return {
        "yxz": fast + x + slow + rest,
        "yzx": fast + slow + x + rest,
        "zyx": slow + fast + x + rest,
        "zxy": slow + x + fast + rest,
        "xyz": x + dp,
    }


def swap(value, bit):
    axis, place = bit
    pairs = [(p, p ^ (1 << place)) for p in range(lax.axis_size(axis))]
    return lax.ppermute(value, axis, pairs)


def add_low(*terms):
    total = terms[0].astype(F32)
    for term in terms[1:]:
        total = total + term.astype(F32)
    return total.astype(terms[0].dtype)


def halvings(kept, sent, bits):
    steps = [(kept, sent)]
    for bit in bits:
        received = swap(sent, bit)
        kept, sent = add_low(kept[0], received[0]), add_low(kept[1], received[1])
        steps.append((kept, sent))
    return steps


def last_sum(step, bit):
    kept, sent = step
    return kept.astype(F32) + swap(sent, bit).astype(F32)


def behind(kernel, start, count):
    return lambda *refs: kernel(*refs[:start], *refs[start + count :])


def dot(left, right, dims=NN):
    return lax.dot_general(left, right, dims, preferred_element_type=F32)


def normalize(values):
    centred = values - jnp.mean(values, axis=-1, keepdims=True)
    root = lax.rsqrt(jnp.mean(centred * centred, axis=-1, keepdims=True) + EPSILON)
    return centred * root, root


def norm_low(values, gain):
    return (normalize(values)[0] * gain).astype(BF16)


def norm_back(values, gain, grad):
    hat, root = normalize(values)
    scaled = grad * gain
    along = jnp.mean(scaled * hat, axis=-1, keepdims=True)
    back = root * (scaled - jnp.mean(scaled, axis=-1, keepdims=True) - hat * along)
    parts = grad * hat
    return back, parts.reshape(parts.shape[0] // 8, 8, parts.shape[1]).sum(0)


def pack_stat(stat):
    lane = lax.broadcasted_iota(jnp.int32, stat.shape, 1)
    high = stat.astype(BF16).astype(F32)
    middle = (stat - high).astype(BF16).astype(F32)
    low = stat - high - middle
    packed = jnp.where(lane < HEADS, high, pltpu.roll(middle, HEADS, 1))
    packed = jnp.where(lane < 2 * HEADS, packed, pltpu.roll(low, 2 * HEADS, 1))
    return jnp.where(lane < 3 * HEADS, packed, 0.0)


def pack_rows(stats):
    pieces = []
    for stat in stats:
        high = stat.astype(BF16).astype(F32)
        middle = (stat - high).astype(BF16).astype(F32)
        pieces += [high, middle, stat - high - middle]
    empty = jnp.zeros((LANES - HEADS * len(pieces), pieces[0].shape[1]), F32)
    return jnp.concatenate(pieces + [empty], axis=0).T


def unpack_stat(packed):
    full = packed.astype(F32)
    return (
        full + pltpu.roll(full, LANES - HEADS, 1) + pltpu.roll(full, LANES - 2 * HEADS, 1)
    )


def head(index, base=0):
    return slice(base + index * LANES, base + (index + 1) * LANES)


def merge(first, second, width):
    first_stat = unpack_stat(first[:, width:])
    second_stat = unpack_stat(second[:, width:])
    top = jnp.maximum(first_stat, second_stat)
    first_weight = jnp.exp2(first_stat - top)
    second_weight = jnp.exp2(second_stat - top)
    total = first_weight + second_weight
    first_weight = first_weight / total
    second_weight = second_weight / total
    mixed = [
        first[:, head(h)].astype(F32) * first_weight[:, h : h + 1]
        + second[:, head(h)].astype(F32) * second_weight[:, h : h + 1]
        for h in range(HEADS)
    ]
    return mixed, top + jnp.log2(total)


def params(limit=56):
    return pltpu.CompilerParams(vmem_limit_bytes=limit * MIB)


def cost(micros):
    return pl.CostEstimate(
        flops=int(micros * FLOPS_PER_MICRO), bytes_accessed=0, transcendentals=0
    )


def shape_of(shape, dtype):
    return jax.ShapeDtypeStruct(shape, dtype)


def pix_project_kernel(pix_ref, gain_ref, weight_ref, low_ref, kv_ref):
    low = norm_low(pix_ref[...].astype(F32), gain_ref[...])
    low_ref[...] = low
    kv_ref[...] = dot(low, weight_ref[...]).astype(BF16)


def pix_project(pixels, gain, weight, after):
    rows, width = pixels.shape
    wide = weight.shape[1]
    block = 384 if rows % 384 == 0 else 128
    return pl.pallas_call(
        behind(pix_project_kernel, 3, len(after)),
        grid=(rows // block,),
        in_specs=[
            pl.BlockSpec((block, width), lambda i: (i, 0)),
            pl.BlockSpec((1, width), lambda i: (0, 0)),
            pl.BlockSpec((width, wide), lambda i: (0, 0)),
        ]
        + [ANY] * len(after),
        out_specs=[
            pl.BlockSpec((block, width), lambda i: (i, 0)),
            pl.BlockSpec((block, wide), lambda i: (i, 0)),
        ],
        out_shape=[shape_of((rows, width), BF16), shape_of((rows, wide), BF16)],
        compiler_params=params(),
        cost_estimate=cost(42),
        name="pix_project",
    )(pixels, gain, weight, *after)


def cross_forward_kernel(group_ref, count_ref, query_ref, kv_ref, out_ref):
    count = count_ref[group_ref[pl.program_id(0)]]
    width = query_ref.shape[2]
    slots = kv_ref.shape[1]
    valid = lax.broadcasted_iota(jnp.int32, (slots, 1), 0) < count
    ones = jnp.ones((slots, LANES), BF16)
    heads = range(HEADS)
    scores = [
        jnp.where(
            valid,
            dot(kv_ref[0, :, head(h)], query_ref[0, :, head(h)], NT) * (SCALE * LOG2_E),
            EMPTY,
        )
        for h in heads
    ]
    tops = [jnp.max(s, axis=0, keepdims=True) for s in scores]
    expos = [jnp.exp2(s - t) for s, t in zip(scores, tops)]
    totals = [jnp.sum(e, axis=0, keepdims=True) for e in expos]
    expos = [e.astype(BF16) for e in expos]
    for h in heads:
        values = jnp.concatenate([kv_ref[0, :, head(h, width)], ones], axis=1)
        mixed = dot(expos[h], values, TN)
        out_ref[0, :, head(h)] = (mixed[:, :LANES] * (1.0 / mixed[:, LANES:])).astype(BF16)
    stat = jnp.concatenate(tops, axis=0) + jnp.log2(jnp.concatenate(totals, axis=0))
    out_ref[0, :, width:] = pack_rows([stat]).astype(BF16)


def cross_forward(groups, counts, query, kv, after):
    number, rows, width = query.shape
    slots, wide = kv.shape[1:]
    return pl.pallas_call(
        behind(cross_forward_kernel, 4, len(after)),
        grid_spec=pltpu.PrefetchScalarGridSpec(
            num_scalar_prefetch=2,
            grid=(number,),
            in_specs=[
                pl.BlockSpec((1, rows, width), lambda i, g, n: (i, 0, 0)),
                pl.BlockSpec((1, slots, wide), lambda i, g, n: (g[i], 0, 0)),
            ]
            + [ANY] * len(after),
            out_specs=pl.BlockSpec((1, rows, width + LANES), lambda i, g, n: (i, 0, 0)),
        ),
        out_shape=shape_of((number, rows, width + LANES), BF16),
        compiler_params=params(),
        cost_estimate=cost(12),
        name="cross_forward",
    )(groups, counts, query, kv, *after)


def merge_kernel(first_ref, second_ref, out_ref):
    width = out_ref.shape[2] - LANES
    mixed, stat = merge(first_ref[0], second_ref[0], width)
    for h in range(HEADS):
        out_ref[0, :, head(h)] = mixed[h].astype(BF16)
    out_ref[0, :, width:] = pack_stat(stat).astype(BF16)


def merge_call(first, second):
    number, rows, wide = first.shape
    spec = pl.BlockSpec((1, rows, wide), lambda i: (i, 0, 0))
    return pl.pallas_call(
        merge_kernel,
        grid=(number,),
        in_specs=[spec, spec],
        out_specs=spec,
        out_shape=shape_of(first.shape, BF16),
        compiler_params=params(),
        cost_estimate=cost(3),
        name="merge",
    )(first, second)


def cross_backward_kernel(group_ref, count_ref, query_ref, grad_ref, kv_ref, dq_ref, dkv_ref):
    count = count_ref[group_ref[pl.program_id(0)]]
    width = query_ref.shape[2]
    slots = kv_ref.shape[1]
    valid = lax.broadcasted_iota(jnp.int32, (slots, 1), 0) < count
    stat = grad_ref[0, :, width:].astype(F32).T
    pieces = [stat[HEADS * i : HEADS * (i + 1)] for i in range(6)]
    log_total = pieces[0] + pieces[1] + pieces[2]
    delta = pieces[3] + pieces[4] + pieces[5]
    heads = range(HEADS)
    scores = [
        dot(kv_ref[0, :, head(h)], query_ref[0, :, head(h)], NT) * (SCALE * LOG2_E)
        - log_total[h : h + 1]
        for h in heads
    ]
    probs = [jnp.where(valid, jnp.exp2(s), 0.0) for s in scores]
    d_probs = [dot(kv_ref[0, :, head(h, width)], grad_ref[0, :, head(h)], NT) for h in heads]
    d_scores = [(probs[h] * (d_probs[h] - delta[h : h + 1])).astype(BF16) for h in heads]
    probs = [p.astype(BF16) for p in probs]
    for h in heads:
        dkv_ref[0, :, head(h)] = (dot(d_scores[h], query_ref[0, :, head(h)]) * SCALE).astype(BF16)
        dkv_ref[0, :, head(h, width)] = dot(probs[h], grad_ref[0, :, head(h)]).astype(BF16)
        dq_ref[0, :, head(h)] = (dot(d_scores[h], kv_ref[0, :, head(h)], TN) * SCALE).astype(BF16)


def cross_backward(groups, counts, query, grad, kv, old, after):
    number, rows, width = query.shape
    slots, wide = kv.shape[1:]
    olds = [] if old is None else [old]
    extra = olds + list(after)
    return pl.pallas_call(
        behind(cross_backward_kernel, 5, len(extra)),
        grid_spec=pltpu.PrefetchScalarGridSpec(
            num_scalar_prefetch=2,
            grid=(number,),
            in_specs=[
                pl.BlockSpec((1, rows, width), lambda i, g, n: (i, 0, 0)),
                pl.BlockSpec((1, rows, width + LANES), lambda i, g, n: (i, 0, 0)),
                pl.BlockSpec((1, slots, wide), lambda i, g, n: (g[i], 0, 0)),
            ]
            + [ANY] * len(extra),
            out_specs=[
                pl.BlockSpec((1, rows, width), lambda i, g, n: (i, 0, 0)),
                pl.BlockSpec((1, slots, wide), lambda i, g, n: (g[i], 0, 0)),
            ],
        ),
        out_shape=[shape_of((number, rows, width), BF16), shape_of(kv.shape, BF16)],
        input_output_aliases={} if old is None else {5: 1},
        compiler_params=params(),
        cost_estimate=cost(3.5),
        name="cross_backward",
    )(groups, counts, query, grad, kv, *extra)


def pix_back_kernel(dkv_ref, weight_ref, pix_ref, gain_ref, out_ref):
    back, _ = norm_back(
        pix_ref[...].astype(F32), gain_ref[...], dot(dkv_ref[...], weight_ref[...], NT)
    )
    out_ref[...] = back.astype(BF16)


def pix_back(dkv, weight, pixels, gain, after):
    rows, width = pixels.shape
    wide = weight.shape[1]
    block = 384 if rows % 384 == 0 else 128
    return pl.pallas_call(
        behind(pix_back_kernel, 4, len(after)),
        grid=(rows // block,),
        in_specs=[
            pl.BlockSpec((block, wide), lambda i: (i, 0)),
            pl.BlockSpec((width, wide), lambda i: (0, 0)),
            pl.BlockSpec((block, width), lambda i: (i, 0)),
            pl.BlockSpec((1, width), lambda i: (0, 0)),
        ]
        + [ANY] * len(after),
        out_specs=pl.BlockSpec((block, width), lambda i: (i, 0)),
        out_shape=shape_of((rows, width), BF16),
        compiler_params=params(),
        cost_estimate=cost(11),
        name="pix_back",
    )(dkv, weight, pixels, gain, *after)


def places(order, second):
    found = []
    rest = order[2:]
    for code in range(2 ** (len(order) - 1)):
        first, spot = code & 1, tuple((code >> (1 + k)) & 1 for k in range(len(rest)))
        offset = {"dp": 0, "pix": 0}
        for bit, on in [(order[0], first)] + list(zip(rest, spot)):
            offset[bit[0]] += on << bit[1]
        found.append((first, spot, offset["dp"], offset["pix"]))
    axis, place = order[1]
    moving = second << place
    found.sort(key=lambda entry: (entry[2], entry[3]))
    return found, (moving if axis == "dp" else 0), (moving if axis == "pix" else 0)


def weight_kernel(order, devices, columns, number, sides, fold, here_ref, *refs):
    inputs = 2 * number * sides
    operands, added, outs, scratch = refs[:inputs], refs[inputs:-3], refs[-3:-1], refs[-1]
    found, step_dp, step_pix = places(order, pl.program_id(0))
    for first, spot, dp, pix in found:
        own = here_ref[0] ^ (dp + step_dp)
        block = here_ref[1] ^ (pix + step_pix)
        begin = 0
        for k in range(number):
            tall = operands[2 * k * sides].shape[1] // devices
            width = operands[2 * k * sides + 1].shape[1] // columns
            whole = tall % LANES == 0
            at_rows = own * tall if whole else own * tall // LANES * LANES
            at_rows = pl.ds(pl.multiple_of(at_rows, LANES), max(tall, LANES))
            at_columns = pl.ds(pl.multiple_of(block * width, LANES), width)
            part = None
            for side in range(sides):
                left, right = operands[2 * (k * sides + side) : 2 * (k * sides + side) + 2]
                term = dot(left[:, at_rows], right[:, at_columns], TN)
                part = term if part is None else part + term
            if not whole:
                scratch[:, :width] = part
                inside = pl.multiple_of(lax.rem(own * tall, LANES), tall)
                part = scratch[pl.ds(inside, tall), :width]
            run = tall // fold
            for j in range(fold):
                at = (0,) + spot + (slice(None), slice(begin, begin + width))
                outs[first][at] = part[j * run : (j + 1) * run].astype(BF16)
                begin += width
        for extra in added:
            tall = extra.shape[0] // devices
            at = (0,) + spot + (slice(None), slice(begin, begin + extra.shape[1]))
            rows = pl.ds(pl.multiple_of(own * tall, tall), tall)
            outs[first][at] = extra[rows, :].astype(BF16)
            begin += extra.shape[1]


def weight_blocks(pairs, added, here, order, after, fold=1):
    devices = lax.axis_size("dp")
    columns = lax.axis_size("pix")
    depth = pairs[0][0][0][0].shape[0]
    sides = len(pairs[0][0][0])
    rows = pairs[0][0][1] // devices
    width = sum(right[1] for _, right in pairs) // columns + sum(a.shape[1] for a in added)
    bits = len(order) - 1
    full = (2,) * bits + (rows // fold, width * fold)
    out_spec = pl.BlockSpec((1,) + full[1:], lambda i, h: (i,) + (0,) * (bits + 1))
    arrays, specs = [], []
    for pair in pairs:
        for side in range(sides):
            for group, wide, index in pair:
                arrays.append(group[side])
                specs.append(pl.BlockSpec((depth, wide), lambda i, h, index=index: (0, index)))
    specs += [pl.BlockSpec(array.shape, lambda i, h: (0, 0)) for array in added]
    inputs = arrays + list(added)
    kernel = functools.partial(weight_kernel, order, devices, columns, len(pairs), sides, fold)
    return pl.pallas_call(
        behind(kernel, 1 + len(inputs), len(after)),
        grid_spec=pltpu.PrefetchScalarGridSpec(
            num_scalar_prefetch=1,
            grid=(2,),
            in_specs=specs + [ANY] * len(after),
            out_specs=[out_spec, out_spec],
            scratch_shapes=[pltpu.VMEM((LANES, width), F32)],
        ),
        out_shape=[shape_of(full, BF16)] * 2,
        compiler_params=params(),
        cost_estimate=cost(3.5),
        name="weight_blocks",
    )(here, *inputs, *after)


def pix_weight_kernel(splits, devices, columns, here_ref, left_ref, right_ref, weight_ref, *refs):
    outs, sum_ref, total_ref = refs[:-2], refs[-2], refs[-1]
    step = pl.program_id(0)
    left = left_ref[...]
    wide = total_ref.shape[2]

    def add(first):
        for p in range(columns):
            grad = dot(left, right_ref[:, p * wide : (p + 1) * wide], TN)
            total_ref[p] = grad if first else total_ref[p] + grad

    pl.when(step == 0)(lambda: add(True))
    pl.when(step > 0)(lambda: add(False))

    @pl.when(step == pl.num_programs(0) - 1)
    def _():
        height = left_ref.shape[1] // devices
        width = wide // len(splits)
        sums = jnp.zeros(sum_ref.shape, F32)
        for p in range(columns):
            for h in range(wide // LANES):
                weight = weight_ref[:, head(h, p * wide)].astype(F32)
                sums = sums + total_ref[p, :, head(h)] * weight
        sum_ref[...] = sums
        for k, order in enumerate(splits):
            for second in range(2):
                found, step_dp, step_pix = places(order, second)
                for first, spot, dp, pix in found:
                    own = here_ref[0] ^ (dp + step_dp)
                    block = here_ref[1] ^ (pix + step_pix)
                    at_rows = pl.ds(pl.multiple_of(own * height, 32), height)
                    part = total_ref[block, at_rows, k * width : (k + 1) * width]
                    outs[2 * k + first][(second,) + spot] = part.astype(BF16)


def pix_weight(left, right, weight, here, splits, after):
    depth, height = left.shape
    devices = lax.axis_size("dp")
    columns = lax.axis_size("pix")
    wide = right.shape[1]
    width = wide // columns
    bits = len(splits[0]) - 1
    full = (2,) * bits + (height // devices, width // len(splits))
    block = 768 if depth % 768 == 0 else 128
    whole = pl.BlockSpec(full, lambda i, h: (0,) * len(full))
    kernel = functools.partial(pix_weight_kernel, splits, devices, columns)
    return pl.pallas_call(
        behind(kernel, 4, len(after)),
        grid_spec=pltpu.PrefetchScalarGridSpec(
            num_scalar_prefetch=1,
            grid=(depth // block,),
            in_specs=[
                pl.BlockSpec((block, height), lambda i, h: (i, 0)),
                pl.BlockSpec((block, wide), lambda i, h: (i, 0)),
                pl.BlockSpec((height, wide), lambda i, h: (0, 0)),
            ]
            + [ANY] * len(after),
            out_specs=[whole] * (2 * len(splits)) + [pl.BlockSpec((height, LANES), lambda i, h: (0, 0))],
            scratch_shapes=[pltpu.VMEM((columns, height, width), F32)],
        ),
        out_shape=[shape_of(full, BF16)] * (2 * len(splits)) + [shape_of((height, LANES), F32)],
        compiler_params=params(),
        cost_estimate=cost(11),
        name="pix_weight",
    )(here, left, right, weight, *after)


def query_kernel(lat_ref, gain_ref, weight_ref, low_ref, query_ref):
    low = norm_low(lat_ref[...].astype(F32), gain_ref[...])
    low_ref[...] = low
    query_ref[...] = dot(low, weight_ref[...]).astype(BF16)


def query_project(latents, gain, weight):
    rows, width = latents.shape
    return pl.pallas_call(
        query_kernel,
        out_shape=[shape_of((rows, width), BF16)] * 2,
        compiler_params=params(),
        cost_estimate=cost(3.5),
        name="query_project",
    )(latents, gain, weight)


def latent_end_kernel(count, *refs):
    terms = refs[:count]
    (
        lat_ref,
        gain_ref,
        weight_ref,
        d_first_ref,
        pix_gain_ref,
        pix_rows_ref,
        self_sum_ref,
        mlp_sum_ref,
        query_ref,
        out_ref,
        gains_ref,
    ) = refs[count:]
    total = terms[0][...].astype(F32)
    for term in terms[1:]:
        total = total + term[...].astype(F32)
    low = total.astype(BF16)
    query_ref[...] = low
    back, lat_sum = norm_back(
        lat_ref[...].astype(F32), gain_ref[...], dot(low, weight_ref[...], NT)
    )
    out_ref[...] = d_first_ref[...] + back
    sums = [jnp.sum(s, axis=0, keepdims=True) for s in (lat_sum, self_sum_ref[...], mlp_sum_ref[...])]
    rows = [sums[0], 1.0 / pix_gain_ref[...], sums[1], sums[2]]
    empty = jnp.zeros((LANES - len(rows), rows[0].shape[1]), F32)
    columns = jnp.concatenate(rows + [empty], axis=0).T
    pix_sum = jnp.sum(pix_rows_ref[...], axis=1, keepdims=True)
    lane = lax.broadcasted_iota(jnp.int32, columns.shape, 1)
    gains_ref[...] = jnp.where(lane == 1, columns * pix_sum, columns)


def latent_end(terms, latents, gain, weight, d_first, pix_gain, pix_rows, sums, after):
    rows, width = latents.shape
    vmem = pl.BlockSpec(memory_space=pltpu.VMEM)
    return pl.pallas_call(
        behind(functools.partial(latent_end_kernel, len(terms)), len(terms) + 8, len(after)),
        in_specs=[vmem] * (len(terms) + 8) + [ANY] * len(after),
        out_specs=[vmem] * 3,
        out_shape=[
            shape_of((rows, width), BF16),
            shape_of((rows, width), F32),
            shape_of((width, LANES), F32),
        ],
        compiler_params=params(),
        cost_estimate=cost(3),
        name="latent_end",
    )(*terms, latents, gain, weight, d_first, pix_gain, pix_rows, *sums, *after)


def start_loads(sources, targets, sems):
    copies = [
        pltpu.make_async_copy(source, target, sems.at[i])
        for i, (source, target) in enumerate(zip(sources, targets))
    ]
    for copy in copies:
        copy.start()
    return copies


def self_softmax(query, keys):
    scores = dot(keys, query, NT) * (SCALE * LOG2_E)
    expo = jnp.exp2(scores - jnp.max(scores, axis=0, keepdims=True))
    return expo * (1.0 / jnp.sum(expo, axis=0, keepdims=True))


def latent_forward_kernel(
    group_rows,
    part_count,
    *refs,
):
    parts = refs[:part_count]
    (
        lat_ref,
        cot_ref,
        self_gain_ref,
        mlp_gain_ref,
        w_cross_hbm,
        w_qkv_hbm,
        w_self_hbm,
        w_in_hbm,
        w_out_hbm,
        acts_ref,
        stat_ref,
        first_ref,
        qkv_ref,
        second_ref,
        out_ref,
        w_cross,
        w_qkv,
        w_self,
        w_in,
        w_out,
        hidden_ref,
        d_act_ref,
        sems,
    ) = refs[part_count:]
    loads = start_loads(
        (w_cross_hbm, w_qkv_hbm, w_self_hbm, w_in_hbm, w_out_hbm),
        (w_cross, w_qkv, w_self, w_in, w_out),
        sems,
    )
    rows, width = lat_ref.shape
    hidden = w_in.shape[1]
    act_ref, d_hidden_ref = (acts_ref.at[:, i * hidden : (i + 1) * hidden] for i in range(2))
    mlp_low_ref, self_low_ref, inner_ref, cross_ref = (
        acts_ref.at[:, 2 * hidden + i * width : 2 * hidden + (i + 1) * width] for i in range(4)
    )
    joined = parts[0][...]
    for i, part in enumerate(parts[1:]):
        mixed, stat = merge(joined, part[...], width)
        if i < part_count - 2:
            joined = jnp.concatenate(
                [m.astype(BF16) for m in mixed] + [pack_stat(stat).astype(BF16)], axis=1
            )
    for h in range(HEADS):
        cross_ref[:, head(h)] = mixed[h].astype(BF16)
    stat_ref[...] = stat
    loads[0].wait()
    first = lat_ref[...].astype(F32) + dot(cross_ref[...], w_cross[...])
    first_ref[...] = first
    self_low_ref[...] = norm_low(first, self_gain_ref[...])
    loads[1].wait()
    for part in range(3):
        cols = slice(part * width, (part + 1) * width)
        qkv_ref[:, cols] = dot(self_low_ref[...], w_qkv[:, cols]).astype(BF16)
    spots = [
        (slice(g * group_rows, (g + 1) * group_rows), h)
        for g in range(rows // group_rows)
        for h in range(HEADS)
    ]
    probs = [
        self_softmax(qkv_ref[at, head(h)], qkv_ref[at, head(h, width)]).astype(BF16)
        for at, h in spots
    ]
    for (at, h), p in zip(spots, probs):
        inner_ref[at, head(h)] = dot(p, qkv_ref[at, head(h, 2 * width)], TN).astype(BF16)
    loads[2].wait()
    second = first_ref[...] + dot(inner_ref[...], w_self[...])
    second_ref[...] = second
    mlp_low_ref[...] = norm_low(second, mlp_gain_ref[...])
    loads[3].wait()
    loads[4].wait()
    chunk = hidden_ref.shape[2]
    chunks = w_in.shape[1] // chunk

    def multiply(i, slot):
        at = pl.ds(pl.multiple_of(i * chunk, chunk), chunk)
        hidden_ref[slot] = dot(mlp_low_ref[...], w_in[:, at])
        d_act_ref[slot] = dot(cot_ref[...], w_out[at, :], NT)

    def activate(i, slot):
        at = pl.ds(pl.multiple_of(i * chunk, chunk), chunk)
        hidden = hidden_ref[slot]
        gate = 0.5 + 0.5 * lax.erf(hidden * 0.5**0.5)
        bell = jnp.exp2((-0.5 * LOG2_E) * hidden * hidden) * 0.3989422804014327
        act_ref[:, at] = (hidden * gate).astype(BF16)
        d_hidden_ref[:, at] = (d_act_ref[slot] * (gate + hidden * bell)).astype(BF16)

    multiply(0, 0)

    def step(i, carry):
        slot = lax.rem(i, 2)
        multiply(i + 1, 1 - slot)
        activate(i, slot)
        return carry

    lax.fori_loop(0, chunks - 1, step, 0)
    activate(chunks - 1, (chunks - 1) % 2)
    out_ref[...] = (second_ref[...] + dot(act_ref[...], w_out[...])).astype(BF16)


def latent_forward(parts, group_rows, latents, cot, self_gain, mlp_gain, weights, after):
    rows, width = latents.shape
    hidden = weights[3].shape[1]
    vmem = pl.BlockSpec(memory_space=pltpu.VMEM)
    return pl.pallas_call(
        behind(
            functools.partial(latent_forward_kernel, group_rows, len(parts)),
            len(parts) + 9,
            len(after),
        ),
        in_specs=[vmem] * (len(parts) + 4) + [ANY] * (5 + len(after)),
        out_specs=[vmem] * 6,
        out_shape=[
            shape_of((rows, 2 * hidden + 4 * width), BF16),
            shape_of((rows, LANES), F32),
            shape_of((rows, width), F32),
            shape_of((rows, 3 * width), BF16),
            shape_of((rows, width), F32),
            shape_of((rows, width), BF16),
        ],
        scratch_shapes=[pltpu.VMEM(w.shape, BF16) for w in weights]
        + [pltpu.VMEM((2, rows, 512), F32)] * 2
        + [pltpu.SemaphoreType.DMA((5,))],
        compiler_params=params(),
        cost_estimate=cost(20),
        name="latent_forward",
    )(*parts, latents, cot, self_gain, mlp_gain, *weights, *after)


def latent_backward_kernel(
    group_rows,
    acts_hbm,
    cot_ref,
    second_ref,
    first_ref,
    qkv_ref,
    stat_ref,
    self_gain_ref,
    mlp_gain_ref,
    w_in_hbm,
    w_self_hbm,
    w_qkv_hbm,
    w_cross_hbm,
    grads_ref,
    d_first_ref,
    d_cross_ref,
    mlp_sum_ref,
    self_sum_ref,
    w_in,
    w_self,
    w_qkv,
    w_cross,
    d_inner,
    d_hidden_ref,
    cross_ref,
    sems,
):
    rows, width = cot_ref.shape
    hidden = d_hidden_ref.shape[1]
    loads = start_loads(
        (
            acts_hbm.at[:, hidden : 2 * hidden],
            w_in_hbm,
            w_self_hbm,
            w_qkv_hbm,
            w_cross_hbm,
            acts_hbm.at[:, 2 * hidden + 3 * width : 2 * hidden + 4 * width],
        ),
        (d_hidden_ref, w_in, w_self, w_qkv, w_cross, cross_ref),
        sems,
    )
    d_qkv_ref = grads_ref.at[:, : 3 * width]
    d_second_low_ref = grads_ref.at[:, 3 * width : 4 * width]
    d_first_low_ref = grads_ref.at[:, 4 * width :]
    loads[0].wait()
    loads[1].wait()
    back, mlp_sum_ref[...] = norm_back(
        second_ref[...], mlp_gain_ref[...], dot(d_hidden_ref[...], w_in[...], NT)
    )
    d_second = cot_ref[...].astype(F32) + back
    d_first_ref[...] = d_second
    d_second_low_ref[...] = d_second.astype(BF16)
    loads[2].wait()
    d_inner[...] = dot(d_second_low_ref[...], w_self[...], NT).astype(BF16)
    for g in range(rows // group_rows):
        at = slice(g * group_rows, (g + 1) * group_rows)
        heads = range(HEADS)
        probs = [self_softmax(qkv_ref[at, head(h)], qkv_ref[at, head(h, width)]) for h in heads]
        d_probs = [dot(qkv_ref[at, head(h, 2 * width)], d_inner[at, head(h)], NT) for h in heads]
        alongs = [jnp.sum(p * d, axis=0, keepdims=True) for p, d in zip(probs, d_probs)]
        d_scores = [(p * (d - a)).astype(BF16) for p, d, a in zip(probs, d_probs, alongs)]
        for h in heads:
            query = qkv_ref[at, head(h)]
            keys = qkv_ref[at, head(h, width)]
            d_qkv_ref[at, head(h)] = (dot(d_scores[h], keys, TN) * SCALE).astype(BF16)
            d_qkv_ref[at, head(h, width)] = (dot(d_scores[h], query) * SCALE).astype(BF16)
            d_qkv_ref[at, head(h, 2 * width)] = dot(
                probs[h].astype(BF16), d_inner[at, head(h)]
            ).astype(BF16)
    loads[3].wait()
    back, self_sum_ref[...] = norm_back(
        first_ref[...], self_gain_ref[...], dot(d_qkv_ref[...], w_qkv[...], NT)
    )
    d_first = d_first_ref[...] + back
    d_first_ref[...] = d_first
    d_first_low_ref[...] = d_first.astype(BF16)
    loads[4].wait()
    loads[5].wait()
    d_cross = dot(d_first_low_ref[...], w_cross[...], NT).astype(BF16)
    d_cross_ref[:, :width] = d_cross
    lane = lax.broadcasted_iota(jnp.int32, (rows, LANES), 1)
    delta = jnp.zeros((rows, LANES), F32)
    for h in range(HEADS):
        along = d_cross[:, head(h)].astype(F32) * cross_ref[:, head(h)].astype(F32)
        delta = jnp.where(lane == h, jnp.sum(along, axis=-1, keepdims=True), delta)
    packed = pack_stat(stat_ref[...]) + pltpu.roll(pack_stat(delta), 3 * HEADS, 1)
    d_cross_ref[:, width:] = packed.astype(BF16)


def latent_backward(group_rows, acts, arrays, weights, after):
    rows, width = arrays[0].shape
    vmem = pl.BlockSpec(memory_space=pltpu.VMEM)
    return pl.pallas_call(
        behind(
            functools.partial(latent_backward_kernel, group_rows), len(arrays) + 5, len(after)
        ),
        in_specs=[ANY] + [vmem] * len(arrays) + [ANY] * (4 + len(after)),
        out_specs=[vmem] * 5,
        out_shape=[
            shape_of((rows, 5 * width), BF16),
            shape_of((rows, width), F32),
            shape_of((rows, width + LANES), BF16),
            shape_of((8, width), F32),
            shape_of((8, width), F32),
        ],
        scratch_shapes=[pltpu.VMEM(w.shape, BF16) for w in weights]
        + [
            pltpu.VMEM((rows, width), BF16),
            pltpu.VMEM((rows, weights[0].shape[1]), BF16),
            pltpu.VMEM((rows, width), BF16),
            pltpu.SemaphoreType.DMA((6,)),
        ],
        compiler_params=params(),
        cost_estimate=cost(15.5),
        name="latent_backward",
    )(acts, *arrays, *weights, *after)


def shards(
    latents,
    pixels,
    pixel_mask,
    cotangent,
    lat_gain,
    pix_gain,
    self_gain,
    mlp_gain,
    w_query,
    w_kv,
    w_cross_out,
    w_qkv,
    w_self_out,
    w_mlp_in,
    w_mlp_out,
):
    own, group_rows, width = latents.shape
    groups, slots = pixel_mask.shape
    rows = own * group_rows
    lat_rows = latents.reshape(rows, width)
    cot_rows = cotangent.reshape(rows, width)
    pix_rows = pixels.reshape(groups * slots, width)
    gain_rows = [g.reshape(1, width) for g in (lat_gain, pix_gain, self_gain, mlp_gain)]
    lat_gain, pix_gain, self_gain, mlp_gain = gain_rows
    counts = jnp.sum(pixel_mask, axis=1, dtype=jnp.int32)
    order = orders()
    pix_here = lax.axis_index("pix").astype(jnp.int32)
    dp_here = lax.axis_index("dp").astype(jnp.int32)
    here = jnp.stack([dp_here, pix_here])

    holders = lax.axis_size("pix")
    of_holder = [
        jnp.stack([(pix_here ^ r) * own + i for i in range(own)]).astype(jnp.int32)
        for r in range(holders)
    ]
    ranked = list(range(2, holders)) + [1, 0]

    def hop(value, distance):
        pairs = [(p, p ^ distance) for p in range(holders)]
        return value if distance == 0 else lax.ppermute(value, "pix", pairs)

    lat_low, query = query_project(lat_rows, lat_gain, w_query)
    query = query.reshape(own, group_rows, width)
    queries = [hop(query, r - r % 2) for r in range(holders)]
    queries = [swap(q, CORE) if r % 2 else q for r, q in enumerate(queries)]
    pix_low, kv_rows = pix_project(pix_rows, pix_gain, w_kv, [query])
    kv = kv_rows.reshape(groups, slots, 2 * width)

    mixed = {}
    last = []
    for r in ranked:
        if r == 1:
            joined = {
                far: merge_call(mixed[far], swap(mixed[far + 1], CORE))
                for far in range(2, holders, 2)
            }
            last = list(joined.values())
        mixed[r] = cross_forward(of_holder[r], counts, queries[r], kv, last)
        last = [mixed[r]]
    parts = [mixed[0], swap(mixed[1], CORE)] + [hop(joined[far], far) for far in joined]
    parts = [part.reshape(rows, width + LANES) for part in parts]

    both_cot = (cot_rows, swap(cot_rows, CORE))
    acts, cross_stat, first, qkv, second, latents_out = latent_forward(
        parts,
        group_rows,
        lat_rows,
        cot_rows,
        self_gain,
        mlp_gain,
        (w_cross_out, w_qkv, w_self_out, w_mlp_in, w_mlp_out),
        [both_cot[1]],
    )
    grads_low, d_first, d_cross, mlp_sum, self_sum = latent_backward(
        group_rows,
        acts,
        (cot_rows, second, first, qkv, cross_stat, self_gain, mlp_gain),
        (w_mlp_in, w_self_out, w_qkv, w_cross_out),
        [],
    )
    d_cross = d_cross.reshape(own, group_rows, width + LANES)
    grads = {0: d_cross, 1: swap(d_cross, CORE)}
    for far in range(2, holders, 2):
        grads[far] = hop(d_cross, far)
        grads[far + 1] = swap(grads[far], CORE)

    both_acts = (acts, swap(acts, CORE))
    both_grads = (grads_low, swap(grads_low, CORE))
    wide = w_mlp_in.shape[1]
    low_at = 2 * wide // width
    fold = wide // width
    out_parts = weight_blocks(
        [((both_acts, wide, 0), (both_cot, width, 0))], [], here, order["yzx"], [grads_low], fold
    )
    in_parts = weight_blocks(
        [((both_acts, width, low_at), (both_acts, wide, 1))], [], here, order["zyx"], out_parts
    )
    out_steps = halvings(*out_parts, order["yzx"][:2])
    in_steps = halvings(*in_parts, order["zyx"][:2])
    mlp_parts = [jnp.concatenate(pair, axis=-1) for pair in zip(out_steps[2], in_steps[2])]
    mlp_steps = halvings(*mlp_parts, order["yzx"][2:-1])
    mlp_total = last_sum(mlp_steps[-1], order["yzx"][-1])
    self_pairs = [
        ((both_acts, width, low_at + 2), (both_grads, width, 3)),
        ((both_acts, width, low_at + 1), (both_grads, 3 * width, 0)),
        ((both_acts, width, low_at + 3), (both_grads, width, 4)),
    ]
    self_parts = weight_blocks(self_pairs, [], here, order["xyz"], in_parts)
    self_steps = halvings(*self_parts, order["xyz"][:-1])
    self_total = last_sum(self_steps[-1], order["xyz"][-1])
    dqs = {}
    d_kv, last = None, self_parts
    far_terms = []
    for far in range(2, holders, 2):
        for r in (far, far + 1):
            dqs[r], d_kv = cross_backward(
                of_holder[r], counts, queries[r], grads[r], kv, d_kv, last
            )
            last = []
        joined_dq = add_low(dqs[far], swap(dqs[far + 1], CORE))
        far_terms.append(hop(joined_dq, far))
        last = [joined_dq]
    dqs[1], d_kv = cross_backward(of_holder[1], counts, queries[1], grads[1], kv, d_kv, [])
    dqs[0], d_kv = cross_backward(of_holder[0], counts, queries[0], grads[0], kv, d_kv, last)
    near_dq = dqs[0].astype(F32) + swap(dqs[1], CORE).astype(F32)
    terms = [near_dq] + far_terms
    terms = [term.reshape(rows, width) for term in terms]
    d_kv_rows = d_kv.reshape(groups * slots, 2 * width)
    splits = [[CORE] + order["zxy"]]
    *kv_parts, kv_rows_sum = pix_weight(
        pix_low, d_kv_rows, w_kv, here, splits, [near_dq, *out_steps[1], *in_steps[1]]
    )
    kv_steps = halvings(*kv_parts, splits[0][:-1])
    kv_total = last_sum(kv_steps[-1], splits[0][-1])
    d_query, d_latents, gains = latent_end(
        terms,
        lat_rows,
        lat_gain,
        w_query,
        d_first,
        pix_gain,
        kv_rows_sum,
        (self_sum, mlp_sum),
        [*self_steps[1], *mlp_parts],
    )
    query_order = [CORE] + order["yxz"]
    query_pairs = [(((lat_low,), width, 0), ((d_query,), width, 0))]
    query_parts = weight_blocks(query_pairs, [gains], here, query_order, kv_steps[1])
    query_steps = halvings(*query_parts, query_order[:-1])
    d_pixels = pix_back(d_kv_rows, w_kv, pix_rows, pix_gain, [*query_parts, *self_steps[2], *mlp_steps[1]])
    split_at = width // holders
    sums = last_sum(query_steps[-1], query_order[-1])
    return (
        latents_out.reshape(latents.shape),
        d_latents.reshape(latents.shape),
        d_pixels.reshape(pixels.shape),
        sums[:, split_at],
        sums[:, split_at + 1],
        sums[:, split_at + 2],
        sums[:, split_at + 3],
        sums[:, :split_at],
        kv_total,
        self_total[:, 4 * split_at :],
        self_total[:, split_at : 4 * split_at],
        self_total[:, :split_at],
        mlp_total[:, fold * split_at :],
        jnp.concatenate(
            [mlp_total[:, j * split_at : (j + 1) * split_at] for j in range(fold)], axis=0
        ),
    )


def solution(mesh):
    held = P(("dp", "pix"), None, None)
    return jax.shard_map(
        shards,
        mesh=mesh,
        in_specs=(held, P("dp", "pix", None), P("dp", "pix"), held) + (P(),) * 11,
        out_specs=(held, held, P("dp", "pix", None)) + (P("dp"),) * 4 + (P("dp", "pix"),) * 7,
        check_vma=False,
    )
```

```python
import functools

import jax
import jax.numpy as jnp
from jax import lax
from jax.experimental import pallas as pl
from jax.experimental.pallas import tpu as pltpu
from jax.sharding import PartitionSpec as P

HEADS = 8
EPSILON = 1e-05
LANES = 128
EMPTY = -1e30
SCALE = LANES**-0.5
LOG2_E = 1.4426950408889634
F32 = jnp.float32
BF16 = jnp.bfloat16
NN = (((1,), (0,)), ((), ()))
NT = (((1,), (1,)), ((), ()))
TN = (((0,), (0,)), ((), ()))
ANY = pl.BlockSpec(memory_space=pl.ANY)
MIB = 1024 * 1024
FLOPS_PER_MICRO = 0.5e9


def bit_count(axis):
    size = lax.axis_size(axis)
    assert size & (size - 1) == 0
    return size.bit_length() - 1


CORE = ("pix", 0)


def orders():
    x = [("pix", i) for i in range(1, bit_count("pix"))]
    dp = [("dp", i) for i in range(bit_count("dp"))]
    fast, slow, rest = dp[:1], dp[1:2], dp[2:]
    return {
        "yxz": fast + x + slow + rest,
        "yzx": fast + slow + x + rest,
        "zyx": slow + fast + x + rest,
        "zxy": slow + x + fast + rest,
        "xyz": x + dp,
    }


def swap(value, bit):
    axis, place = bit
    pairs = [(p, p ^ (1 << place)) for p in range(lax.axis_size(axis))]
    return lax.ppermute(value, axis, pairs)


def add_low(*terms):
    total = terms[0].astype(F32)
    for term in terms[1:]:
        total = total + term.astype(F32)
    return total.astype(terms[0].dtype)


def halvings(kept, sent, bits):
    steps = [(kept, sent)]
    for bit in bits:
        received = swap(sent, bit)
        kept, sent = add_low(kept[0], received[0]), add_low(kept[1], received[1])
        steps.append((kept, sent))
    return steps


def last_sum(step, bit):
    kept, sent = step
    return kept.astype(F32) + swap(sent, bit).astype(F32)


def behind(kernel, start, count):
    return lambda *refs: kernel(*refs[:start], *refs[start + count :])


def dot(left, right, dims=NN):
    return lax.dot_general(left, right, dims, preferred_element_type=F32)


def normalize(values):
    centred = values - jnp.mean(values, axis=-1, keepdims=True)
    root = lax.rsqrt(jnp.mean(centred * centred, axis=-1, keepdims=True) + EPSILON)
    return centred * root, root


def norm_low(values, gain):
    return (normalize(values)[0] * gain).astype(BF16)


def norm_back(values, gain, grad):
    hat, root = normalize(values)
    scaled = grad * gain
    along = jnp.mean(scaled * hat, axis=-1, keepdims=True)
    back = root * (scaled - jnp.mean(scaled, axis=-1, keepdims=True) - hat * along)
    parts = grad * hat
    return back, parts.reshape(parts.shape[0] // 8, 8, parts.shape[1]).sum(0)


def pack_stat(stat):
    lane = lax.broadcasted_iota(jnp.int32, stat.shape, 1)
    high = stat.astype(BF16).astype(F32)
    middle = (stat - high).astype(BF16).astype(F32)
    low = stat - high - middle
    packed = jnp.where(lane < HEADS, high, pltpu.roll(middle, HEADS, 1))
    packed = jnp.where(lane < 2 * HEADS, packed, pltpu.roll(low, 2 * HEADS, 1))
    return jnp.where(lane < 3 * HEADS, packed, 0.0)


def pack_rows(stats):
    pieces = []
    for stat in stats:
        high = stat.astype(BF16).astype(F32)
        middle = (stat - high).astype(BF16).astype(F32)
        pieces += [high, middle, stat - high - middle]
    empty = jnp.zeros((LANES - HEADS * len(pieces), pieces[0].shape[1]), F32)
    return jnp.concatenate(pieces + [empty], axis=0).T


def unpack_stat(packed):
    full = packed.astype(F32)
    return (
        full + pltpu.roll(full, LANES - HEADS, 1) + pltpu.roll(full, LANES - 2 * HEADS, 1)
    )


def head(index, base=0):
    return slice(base + index * LANES, base + (index + 1) * LANES)


def merge(first, second, width):
    first_stat = unpack_stat(first[:, width:])
    second_stat = unpack_stat(second[:, width:])
    top = jnp.maximum(first_stat, second_stat)
    first_weight = jnp.exp2(first_stat - top)
    second_weight = jnp.exp2(second_stat - top)
    total = first_weight + second_weight
    first_weight = first_weight / total
    second_weight = second_weight / total
    mixed = [
        first[:, head(h)].astype(F32) * first_weight[:, h : h + 1]
        + second[:, head(h)].astype(F32) * second_weight[:, h : h + 1]
        for h in range(HEADS)
    ]
    return mixed, top + jnp.log2(total)


def params(limit=56):
    return pltpu.CompilerParams(vmem_limit_bytes=limit * MIB)


def cost(micros):
    return pl.CostEstimate(
        flops=int(micros * FLOPS_PER_MICRO), bytes_accessed=0, transcendentals=0
    )


def shape_of(shape, dtype):
    return jax.ShapeDtypeStruct(shape, dtype)


def pix_project_kernel(pix_ref, gain_ref, weight_ref, low_ref, kv_ref):
    low = norm_low(pix_ref[...].astype(F32), gain_ref[...])
    low_ref[...] = low
    kv_ref[...] = dot(low, weight_ref[...]).astype(BF16)


def pix_project(pixels, gain, weight, after):
    rows, width = pixels.shape
    wide = weight.shape[1]
    block = 384 if rows % 384 == 0 else 128
    return pl.pallas_call(
        behind(pix_project_kernel, 3, len(after)),
        grid=(rows // block,),
        in_specs=[
            pl.BlockSpec((block, width), lambda i: (i, 0)),
            pl.BlockSpec((1, width), lambda i: (0, 0)),
            pl.BlockSpec((width, wide), lambda i: (0, 0)),
        ]
        + [ANY] * len(after),
        out_specs=[
            pl.BlockSpec((block, width), lambda i: (i, 0)),
            pl.BlockSpec((block, wide), lambda i: (i, 0)),
        ],
        out_shape=[shape_of((rows, width), BF16), shape_of((rows, wide), BF16)],
        compiler_params=params(),
        cost_estimate=cost(42),
        name="pix_project",
    )(pixels, gain, weight, *after)


def cross_forward_kernel(group_ref, count_ref, query_ref, kv_ref, out_ref):
    count = count_ref[group_ref[pl.program_id(0)]]
    width = query_ref.shape[2]
    slots = kv_ref.shape[1]
    valid = lax.broadcasted_iota(jnp.int32, (slots, 1), 0) < count
    ones = jnp.ones((slots, LANES), BF16)
    heads = range(HEADS)
    scores = [
        jnp.where(
            valid,
            dot(kv_ref[0, :, head(h)], query_ref[0, :, head(h)], NT) * (SCALE * LOG2_E),
            EMPTY,
        )
        for h in heads
    ]
    tops = [jnp.max(s, axis=0, keepdims=True) for s in scores]
    expos = [jnp.exp2(s - t) for s, t in zip(scores, tops)]
    totals = [jnp.sum(e, axis=0, keepdims=True) for e in expos]
    expos = [e.astype(BF16) for e in expos]
    for h in heads:
        values = jnp.concatenate([kv_ref[0, :, head(h, width)], ones], axis=1)
        mixed = dot(expos[h], values, TN)
        out_ref[0, :, head(h)] = (mixed[:, :LANES] * (1.0 / mixed[:, LANES:])).astype(BF16)
    stat = jnp.concatenate(tops, axis=0) + jnp.log2(jnp.concatenate(totals, axis=0))
    out_ref[0, :, width:] = pack_rows([stat]).astype(BF16)


def cross_forward(groups, counts, query, kv, after):
    number, rows, width = query.shape
    slots, wide = kv.shape[1:]
    return pl.pallas_call(
        behind(cross_forward_kernel, 4, len(after)),
        grid_spec=pltpu.PrefetchScalarGridSpec(
            num_scalar_prefetch=2,
            grid=(number,),
            in_specs=[
                pl.BlockSpec((1, rows, width), lambda i, g, n: (i, 0, 0)),
                pl.BlockSpec((1, slots, wide), lambda i, g, n: (g[i], 0, 0)),
            ]
            + [ANY] * len(after),
            out_specs=pl.BlockSpec((1, rows, width + LANES), lambda i, g, n: (i, 0, 0)),
        ),
        out_shape=shape_of((number, rows, width + LANES), BF16),
        compiler_params=params(),
        cost_estimate=cost(12),
        name="cross_forward",
    )(groups, counts, query, kv, *after)


def merge_kernel(first_ref, second_ref, out_ref):
    width = out_ref.shape[2] - LANES
    mixed, stat = merge(first_ref[0], second_ref[0], width)
    for h in range(HEADS):
        out_ref[0, :, head(h)] = mixed[h].astype(BF16)
    out_ref[0, :, width:] = pack_stat(stat).astype(BF16)


def merge_call(first, second):
    number, rows, wide = first.shape
    spec = pl.BlockSpec((1, rows, wide), lambda i: (i, 0, 0))
    return pl.pallas_call(
        merge_kernel,
        grid=(number,),
        in_specs=[spec, spec],
        out_specs=spec,
        out_shape=shape_of(first.shape, BF16),
        compiler_params=params(),
        cost_estimate=cost(3),
        name="merge",
    )(first, second)


def cross_backward_kernel(group_ref, count_ref, query_ref, grad_ref, kv_ref, dq_ref, dkv_ref):
    count = count_ref[group_ref[pl.program_id(0)]]
    width = query_ref.shape[2]
    slots = kv_ref.shape[1]
    valid = lax.broadcasted_iota(jnp.int32, (slots, 1), 0) < count
    stat = grad_ref[0, :, width:].astype(F32).T
    pieces = [stat[HEADS * i : HEADS * (i + 1)] for i in range(6)]
    log_total = pieces[0] + pieces[1] + pieces[2]
    delta = pieces[3] + pieces[4] + pieces[5]
    heads = range(HEADS)
    scores = [
        dot(kv_ref[0, :, head(h)], query_ref[0, :, head(h)], NT) * (SCALE * LOG2_E)
        - log_total[h : h + 1]
        for h in heads
    ]
    probs = [jnp.where(valid, jnp.exp2(s), 0.0) for s in scores]
    d_probs = [dot(kv_ref[0, :, head(h, width)], grad_ref[0, :, head(h)], NT) for h in heads]
    d_scores = [(probs[h] * (d_probs[h] - delta[h : h + 1])).astype(BF16) for h in heads]
    probs = [p.astype(BF16) for p in probs]
    for h in heads:
        dkv_ref[0, :, head(h)] = (dot(d_scores[h], query_ref[0, :, head(h)]) * SCALE).astype(BF16)
        dkv_ref[0, :, head(h, width)] = dot(probs[h], grad_ref[0, :, head(h)]).astype(BF16)
        dq_ref[0, :, head(h)] = (dot(d_scores[h], kv_ref[0, :, head(h)], TN) * SCALE).astype(BF16)


def cross_backward(groups, counts, query, grad, kv, old, after):
    number, rows, width = query.shape
    slots, wide = kv.shape[1:]
    olds = [] if old is None else [old]
    extra = olds + list(after)
    return pl.pallas_call(
        behind(cross_backward_kernel, 5, len(extra)),
        grid_spec=pltpu.PrefetchScalarGridSpec(
            num_scalar_prefetch=2,
            grid=(number,),
            in_specs=[
                pl.BlockSpec((1, rows, width), lambda i, g, n: (i, 0, 0)),
                pl.BlockSpec((1, rows, width + LANES), lambda i, g, n: (i, 0, 0)),
                pl.BlockSpec((1, slots, wide), lambda i, g, n: (g[i], 0, 0)),
            ]
            + [ANY] * len(extra),
            out_specs=[
                pl.BlockSpec((1, rows, width), lambda i, g, n: (i, 0, 0)),
                pl.BlockSpec((1, slots, wide), lambda i, g, n: (g[i], 0, 0)),
            ],
        ),
        out_shape=[shape_of((number, rows, width), BF16), shape_of(kv.shape, BF16)],
        input_output_aliases={} if old is None else {5: 1},
        compiler_params=params(),
        cost_estimate=cost(3.5),
        name="cross_backward",
    )(groups, counts, query, grad, kv, *extra)


def pix_back_kernel(dkv_ref, weight_ref, pix_ref, gain_ref, out_ref):
    back, _ = norm_back(
        pix_ref[...].astype(F32), gain_ref[...], dot(dkv_ref[...], weight_ref[...], NT)
    )
    out_ref[...] = back.astype(BF16)


def pix_back(dkv, weight, pixels, gain, after):
    rows, width = pixels.shape
    wide = weight.shape[1]
    block = 384 if rows % 384 == 0 else 128
    return pl.pallas_call(
        behind(pix_back_kernel, 4, len(after)),
        grid=(rows // block,),
        in_specs=[
            pl.BlockSpec((block, wide), lambda i: (i, 0)),
            pl.BlockSpec((width, wide), lambda i: (0, 0)),
            pl.BlockSpec((block, width), lambda i: (i, 0)),
            pl.BlockSpec((1, width), lambda i: (0, 0)),
        ]
        + [ANY] * len(after),
        out_specs=pl.BlockSpec((block, width), lambda i: (i, 0)),
        out_shape=shape_of((rows, width), BF16),
        compiler_params=params(),
        cost_estimate=cost(11),
        name="pix_back",
    )(dkv, weight, pixels, gain, *after)


def places(order, second):
    found = []
    rest = order[2:]
    for code in range(2 ** (len(order) - 1)):
        first, spot = code & 1, tuple((code >> (1 + k)) & 1 for k in range(len(rest)))
        offset = {"dp": 0, "pix": 0}
        for bit, on in [(order[0], first)] + list(zip(rest, spot)):
            offset[bit[0]] += on << bit[1]
        found.append((first, spot, offset["dp"], offset["pix"]))
    axis, place = order[1]
    moving = second << place
    found.sort(key=lambda entry: (entry[2], entry[3]))
    return found, (moving if axis == "dp" else 0), (moving if axis == "pix" else 0)


def weight_kernel(order, devices, columns, number, sides, fold, here_ref, *refs):
    inputs = 2 * number * sides
    operands, added, outs, scratch = refs[:inputs], refs[inputs:-3], refs[-3:-1], refs[-1]
    found, step_dp, step_pix = places(order, pl.program_id(0))
    for first, spot, dp, pix in found:
        own = here_ref[0] ^ (dp + step_dp)
        block = here_ref[1] ^ (pix + step_pix)
        begin = 0
        for k in range(number):
            tall = operands[2 * k * sides].shape[1] // devices
            width = operands[2 * k * sides + 1].shape[1] // columns
            whole = tall % LANES == 0
            at_rows = own * tall if whole else own * tall // LANES * LANES
            at_rows = pl.ds(pl.multiple_of(at_rows, LANES), max(tall, LANES))
            at_columns = pl.ds(pl.multiple_of(block * width, LANES), width)
            part = None
            for side in range(sides):
                left, right = operands[2 * (k * sides + side) : 2 * (k * sides + side) + 2]
                term = dot(left[:, at_rows], right[:, at_columns], TN)
                part = term if part is None else part + term
            if not whole:
                scratch[:, :width] = part
                inside = pl.multiple_of(lax.rem(own * tall, LANES), tall)
                part = scratch[pl.ds(inside, tall), :width]
            run = tall // fold
            for j in range(fold):
                at = (0,) + spot + (slice(None), slice(begin, begin + width))
                outs[first][at] = part[j * run : (j + 1) * run].astype(BF16)
                begin += width
        for extra in added:
            tall = extra.shape[0] // devices
            at = (0,) + spot + (slice(None), slice(begin, begin + extra.shape[1]))
            rows = pl.ds(pl.multiple_of(own * tall, tall), tall)
            outs[first][at] = extra[rows, :].astype(BF16)
            begin += extra.shape[1]


def weight_blocks(pairs, added, here, order, after, fold=1):
    devices = lax.axis_size("dp")
    columns = lax.axis_size("pix")
    depth = pairs[0][0][0][0].shape[0]
    sides = len(pairs[0][0][0])
    rows = pairs[0][0][1] // devices
    width = sum(right[1] for _, right in pairs) // columns + sum(a.shape[1] for a in added)
    bits = len(order) - 1
    full = (2,) * bits + (rows // fold, width * fold)
    out_spec = pl.BlockSpec((1,) + full[1:], lambda i, h: (i,) + (0,) * (bits + 1))
    arrays, specs = [], []
    for pair in pairs:
        for side in range(sides):
            for group, wide, index in pair:
                arrays.append(group[side])
                specs.append(pl.BlockSpec((depth, wide), lambda i, h, index=index: (0, index)))
    specs += [pl.BlockSpec(array.shape, lambda i, h: (0, 0)) for array in added]
    inputs = arrays + list(added)
    kernel = functools.partial(weight_kernel, order, devices, columns, len(pairs), sides, fold)
    return pl.pallas_call(
        behind(kernel, 1 + len(inputs), len(after)),
        grid_spec=pltpu.PrefetchScalarGridSpec(
            num_scalar_prefetch=1,
            grid=(2,),
            in_specs=specs + [ANY] * len(after),
            out_specs=[out_spec, out_spec],
            scratch_shapes=[pltpu.VMEM((LANES, width), F32)],
        ),
        out_shape=[shape_of(full, BF16)] * 2,
        compiler_params=params(),
        cost_estimate=cost(3.5),
        name="weight_blocks",
    )(here, *inputs, *after)


def pix_weight_kernel(splits, devices, columns, here_ref, left_ref, right_ref, weight_ref, *refs):
    outs, sum_ref, total_ref = refs[:-2], refs[-2], refs[-1]
    step = pl.program_id(0)
    left = left_ref[...]
    wide = total_ref.shape[2]

    def add(first):
        for p in range(columns):
            grad = dot(left, right_ref[:, p * wide : (p + 1) * wide], TN)
            total_ref[p] = grad if first else total_ref[p] + grad

    pl.when(step == 0)(lambda: add(True))
    pl.when(step > 0)(lambda: add(False))

    @pl.when(step == pl.num_programs(0) - 1)
    def _():
        height = left_ref.shape[1] // devices
        width = wide // len(splits)
        sums = jnp.zeros(sum_ref.shape, F32)
        for p in range(columns):
            for h in range(wide // LANES):
                weight = weight_ref[:, head(h, p * wide)].astype(F32)
                sums = sums + total_ref[p, :, head(h)] * weight
        sum_ref[...] = sums
        for k, order in enumerate(splits):
            for second in range(2):
                found, step_dp, step_pix = places(order, second)
                for first, spot, dp, pix in found:
                    own = here_ref[0] ^ (dp + step_dp)
                    block = here_ref[1] ^ (pix + step_pix)
                    at_rows = pl.ds(pl.multiple_of(own * height, 32), height)
                    part = total_ref[block, at_rows, k * width : (k + 1) * width]
                    outs[2 * k + first][(second,) + spot] = part.astype(BF16)


def pix_weight(left, right, weight, here, splits, after):
    depth, height = left.shape
    devices = lax.axis_size("dp")
    columns = lax.axis_size("pix")
    wide = right.shape[1]
    width = wide // columns
    bits = len(splits[0]) - 1
    full = (2,) * bits + (height // devices, width // len(splits))
    block = 768 if depth % 768 == 0 else 128
    whole = pl.BlockSpec(full, lambda i, h: (0,) * len(full))
    kernel = functools.partial(pix_weight_kernel, splits, devices, columns)
    return pl.pallas_call(
        behind(kernel, 4, len(after)),
        grid_spec=pltpu.PrefetchScalarGridSpec(
            num_scalar_prefetch=1,
            grid=(depth // block,),
            in_specs=[
                pl.BlockSpec((block, height), lambda i, h: (i, 0)),
                pl.BlockSpec((block, wide), lambda i, h: (i, 0)),
                pl.BlockSpec((height, wide), lambda i, h: (0, 0)),
            ]
            + [ANY] * len(after),
            out_specs=[whole] * (2 * len(splits)) + [pl.BlockSpec((height, LANES), lambda i, h: (0, 0))],
            scratch_shapes=[pltpu.VMEM((columns, height, width), F32)],
        ),
        out_shape=[shape_of(full, BF16)] * (2 * len(splits)) + [shape_of((height, LANES), F32)],
        compiler_params=params(),
        cost_estimate=cost(11),
        name="pix_weight",
    )(here, left, right, weight, *after)


def query_kernel(lat_ref, gain_ref, weight_ref, low_ref, query_ref):
    low = norm_low(lat_ref[...].astype(F32), gain_ref[...])
    low_ref[...] = low
    query_ref[...] = dot(low, weight_ref[...]).astype(BF16)


def query_project(latents, gain, weight):
    rows, width = latents.shape
    return pl.pallas_call(
        query_kernel,
        out_shape=[shape_of((rows, width), BF16)] * 2,
        compiler_params=params(),
        cost_estimate=cost(3.5),
        name="query_project",
    )(latents, gain, weight)


def latent_end_kernel(count, *refs):
    terms = refs[:count]
    (
        lat_ref,
        gain_ref,
        weight_ref,
        d_first_ref,
        pix_gain_ref,
        pix_rows_ref,
        self_sum_ref,
        mlp_sum_ref,
        query_ref,
        out_ref,
        gains_ref,
    ) = refs[count:]
    total = terms[0][...].astype(F32)
    for term in terms[1:]:
        total = total + term[...].astype(F32)
    low = total.astype(BF16)
    query_ref[...] = low
    back, lat_sum = norm_back(
        lat_ref[...].astype(F32), gain_ref[...], dot(low, weight_ref[...], NT)
    )
    out_ref[...] = d_first_ref[...] + back
    sums = [jnp.sum(s, axis=0, keepdims=True) for s in (lat_sum, self_sum_ref[...], mlp_sum_ref[...])]
    rows = [sums[0], 1.0 / pix_gain_ref[...], sums[1], sums[2]]
    empty = jnp.zeros((LANES - len(rows), rows[0].shape[1]), F32)
    columns = jnp.concatenate(rows + [empty], axis=0).T
    pix_sum = jnp.sum(pix_rows_ref[...], axis=1, keepdims=True)
    lane = lax.broadcasted_iota(jnp.int32, columns.shape, 1)
    gains_ref[...] = jnp.where(lane == 1, columns * pix_sum, columns)


def latent_end(terms, latents, gain, weight, d_first, pix_gain, pix_rows, sums, after):
    rows, width = latents.shape
    vmem = pl.BlockSpec(memory_space=pltpu.VMEM)
    return pl.pallas_call(
        behind(functools.partial(latent_end_kernel, len(terms)), len(terms) + 8, len(after)),
        in_specs=[vmem] * (len(terms) + 8) + [ANY] * len(after),
        out_specs=[vmem] * 3,
        out_shape=[
            shape_of((rows, width), BF16),
            shape_of((rows, width), F32),
            shape_of((width, LANES), F32),
        ],
        compiler_params=params(),
        cost_estimate=cost(3),
        name="latent_end",
    )(*terms, latents, gain, weight, d_first, pix_gain, pix_rows, *sums, *after)


def start_loads(sources, targets, sems):
    copies = [
        pltpu.make_async_copy(source, target, sems.at[i])
        for i, (source, target) in enumerate(zip(sources, targets))
    ]
    for copy in copies:
        copy.start()
    return copies


def self_softmax(query, keys):
    scores = dot(keys, query, NT) * (SCALE * LOG2_E)
    expo = jnp.exp2(scores - jnp.max(scores, axis=0, keepdims=True))
    return expo * (1.0 / jnp.sum(expo, axis=0, keepdims=True))


def latent_forward_kernel(
    group_rows,
    part_count,
    *refs,
):
    parts = refs[:part_count]
    (
        lat_ref,
        cot_ref,
        self_gain_ref,
        mlp_gain_ref,
        w_cross_hbm,
        w_qkv_hbm,
        w_self_hbm,
        w_in_hbm,
        w_out_hbm,
        acts_ref,
        stat_ref,
        first_ref,
        qkv_ref,
        second_ref,
        out_ref,
        w_cross,
        w_qkv,
        w_self,
        w_in,
        w_out,
        hidden_ref,
        d_act_ref,
        sems,
    ) = refs[part_count:]
    loads = start_loads(
        (w_cross_hbm, w_qkv_hbm, w_self_hbm, w_in_hbm, w_out_hbm),
        (w_cross, w_qkv, w_self, w_in, w_out),
        sems,
    )
    rows, width = lat_ref.shape
    hidden = w_in.shape[1]
    act_ref, d_hidden_ref = (acts_ref.at[:, i * hidden : (i + 1) * hidden] for i in range(2))
    mlp_low_ref, self_low_ref, inner_ref, cross_ref = (
        acts_ref.at[:, 2 * hidden + i * width : 2 * hidden + (i + 1) * width] for i in range(4)
    )
    joined = parts[0][...]
    for i, part in enumerate(parts[1:]):
        mixed, stat = merge(joined, part[...], width)
        if i < part_count - 2:
            joined = jnp.concatenate(
                [m.astype(BF16) for m in mixed] + [pack_stat(stat).astype(BF16)], axis=1
            )
    for h in range(HEADS):
        cross_ref[:, head(h)] = mixed[h].astype(BF16)
    stat_ref[...] = stat
    loads[0].wait()
    first = lat_ref[...].astype(F32) + dot(cross_ref[...], w_cross[...])
    first_ref[...] = first
    self_low_ref[...] = norm_low(first, self_gain_ref[...])
    loads[1].wait()
    for part in range(3):
        cols = slice(part * width, (part + 1) * width)
        qkv_ref[:, cols] = dot(self_low_ref[...], w_qkv[:, cols]).astype(BF16)
    spots = [
        (slice(g * group_rows, (g + 1) * group_rows), h)
        for g in range(rows // group_rows)
        for h in range(HEADS)
    ]
    probs = [
        self_softmax(qkv_ref[at, head(h)], qkv_ref[at, head(h, width)]).astype(BF16)
        for at, h in spots
    ]
    for (at, h), p in zip(spots, probs):
        inner_ref[at, head(h)] = dot(p, qkv_ref[at, head(h, 2 * width)], TN).astype(BF16)
    loads[2].wait()
    second = first_ref[...] + dot(inner_ref[...], w_self[...])
    second_ref[...] = second
    mlp_low_ref[...] = norm_low(second, mlp_gain_ref[...])
    loads[3].wait()
    loads[4].wait()
    chunk = hidden_ref.shape[2]
    chunks = w_in.shape[1] // chunk

    def multiply(i, slot):
        at = pl.ds(pl.multiple_of(i * chunk, chunk), chunk)
        hidden_ref[slot] = dot(mlp_low_ref[...], w_in[:, at])
        d_act_ref[slot] = dot(cot_ref[...], w_out[at, :], NT)

    def activate(i, slot):
        at = pl.ds(pl.multiple_of(i * chunk, chunk), chunk)
        hidden = hidden_ref[slot]
        gate = 0.5 + 0.5 * lax.erf(hidden * 0.5**0.5)
        bell = jnp.exp2((-0.5 * LOG2_E) * hidden * hidden) * 0.3989422804014327
        act_ref[:, at] = (hidden * gate).astype(BF16)
        d_hidden_ref[:, at] = (d_act_ref[slot] * (gate + hidden * bell)).astype(BF16)

    multiply(0, 0)

    def step(i, carry):
        slot = lax.rem(i, 2)
        multiply(i + 1, 1 - slot)
        activate(i, slot)
        return carry

    lax.fori_loop(0, chunks - 1, step, 0)
    activate(chunks - 1, (chunks - 1) % 2)
    out_ref[...] = (second_ref[...] + dot(act_ref[...], w_out[...])).astype(BF16)


def latent_forward(parts, group_rows, latents, cot, self_gain, mlp_gain, weights, after):
    rows, width = latents.shape
    hidden = weights[3].shape[1]
    vmem = pl.BlockSpec(memory_space=pltpu.VMEM)
    return pl.pallas_call(
        behind(
            functools.partial(latent_forward_kernel, group_rows, len(parts)),
            len(parts) + 9,
            len(after),
        ),
        in_specs=[vmem] * (len(parts) + 4) + [ANY] * (5 + len(after)),
        out_specs=[vmem] * 6,
        out_shape=[
            shape_of((rows, 2 * hidden + 4 * width), BF16),
            shape_of((rows, LANES), F32),
            shape_of((rows, width), F32),
            shape_of((rows, 3 * width), BF16),
            shape_of((rows, width), F32),
            shape_of((rows, width), BF16),
        ],
        scratch_shapes=[pltpu.VMEM(w.shape, BF16) for w in weights]
        + [pltpu.VMEM((2, rows, 512), F32)] * 2
        + [pltpu.SemaphoreType.DMA((5,))],
        compiler_params=params(),
        cost_estimate=cost(20),
        name="latent_forward",
    )(*parts, latents, cot, self_gain, mlp_gain, *weights, *after)


def latent_backward_kernel(
    group_rows,
    acts_hbm,
    cot_ref,
    second_ref,
    first_ref,
    qkv_ref,
    stat_ref,
    self_gain_ref,
    mlp_gain_ref,
    w_in_hbm,
    w_self_hbm,
    w_qkv_hbm,
    w_cross_hbm,
    grads_ref,
    d_first_ref,
    d_cross_ref,
    mlp_sum_ref,
    self_sum_ref,
    w_in,
    w_self,
    w_qkv,
    w_cross,
    d_inner,
    d_hidden_ref,
    cross_ref,
    sems,
):
    rows, width = cot_ref.shape
    hidden = d_hidden_ref.shape[1]
    loads = start_loads(
        (
            acts_hbm.at[:, hidden : 2 * hidden],
            w_in_hbm,
            w_self_hbm,
            w_qkv_hbm,
            w_cross_hbm,
            acts_hbm.at[:, 2 * hidden + 3 * width : 2 * hidden + 4 * width],
        ),
        (d_hidden_ref, w_in, w_self, w_qkv, w_cross, cross_ref),
        sems,
    )
    d_qkv_ref = grads_ref.at[:, : 3 * width]
    d_second_low_ref = grads_ref.at[:, 3 * width : 4 * width]
    d_first_low_ref = grads_ref.at[:, 4 * width :]
    loads[0].wait()
    loads[1].wait()
    back, mlp_sum_ref[...] = norm_back(
        second_ref[...], mlp_gain_ref[...], dot(d_hidden_ref[...], w_in[...], NT)
    )
    d_second = cot_ref[...].astype(F32) + back
    d_first_ref[...] = d_second
    d_second_low_ref[...] = d_second.astype(BF16)
    loads[2].wait()
    d_inner[...] = dot(d_second_low_ref[...], w_self[...], NT).astype(BF16)
    for g in range(rows // group_rows):
        at = slice(g * group_rows, (g + 1) * group_rows)
        heads = range(HEADS)
        probs = [self_softmax(qkv_ref[at, head(h)], qkv_ref[at, head(h, width)]) for h in heads]
        d_probs = [dot(qkv_ref[at, head(h, 2 * width)], d_inner[at, head(h)], NT) for h in heads]
        alongs = [jnp.sum(p * d, axis=0, keepdims=True) for p, d in zip(probs, d_probs)]
        d_scores = [(p * (d - a)).astype(BF16) for p, d, a in zip(probs, d_probs, alongs)]
        for h in heads:
            query = qkv_ref[at, head(h)]
            keys = qkv_ref[at, head(h, width)]
            d_qkv_ref[at, head(h)] = (dot(d_scores[h], keys, TN) * SCALE).astype(BF16)
            d_qkv_ref[at, head(h, width)] = (dot(d_scores[h], query) * SCALE).astype(BF16)
            d_qkv_ref[at, head(h, 2 * width)] = dot(
                probs[h].astype(BF16), d_inner[at, head(h)]
            ).astype(BF16)
    loads[3].wait()
    back, self_sum_ref[...] = norm_back(
        first_ref[...], self_gain_ref[...], dot(d_qkv_ref[...], w_qkv[...], NT)
    )
    d_first = d_first_ref[...] + back
    d_first_ref[...] = d_first
    d_first_low_ref[...] = d_first.astype(BF16)
    loads[4].wait()
    loads[5].wait()
    d_cross = dot(d_first_low_ref[...], w_cross[...], NT).astype(BF16)
    d_cross_ref[:, :width] = d_cross
    lane = lax.broadcasted_iota(jnp.int32, (rows, LANES), 1)
    delta = jnp.zeros((rows, LANES), F32)
    for h in range(HEADS):
        along = d_cross[:, head(h)].astype(F32) * cross_ref[:, head(h)].astype(F32)
        delta = jnp.where(lane == h, jnp.sum(along, axis=-1, keepdims=True), delta)
    packed = pack_stat(stat_ref[...]) + pltpu.roll(pack_stat(delta), 3 * HEADS, 1)
    d_cross_ref[:, width:] = packed.astype(BF16)


def latent_backward(group_rows, acts, arrays, weights, after):
    rows, width = arrays[0].shape
    vmem = pl.BlockSpec(memory_space=pltpu.VMEM)
    return pl.pallas_call(
        behind(
            functools.partial(latent_backward_kernel, group_rows), len(arrays) + 5, len(after)
        ),
        in_specs=[ANY] + [vmem] * len(arrays) + [ANY] * (4 + len(after)),
        out_specs=[vmem] * 5,
        out_shape=[
            shape_of((rows, 5 * width), BF16),
            shape_of((rows, width), F32),
            shape_of((rows, width + LANES), BF16),
            shape_of((8, width), F32),
            shape_of((8, width), F32),
        ],
        scratch_shapes=[pltpu.VMEM(w.shape, BF16) for w in weights]
        + [
            pltpu.VMEM((rows, width), BF16),
            pltpu.VMEM((rows, weights[0].shape[1]), BF16),
            pltpu.VMEM((rows, width), BF16),
            pltpu.SemaphoreType.DMA((6,)),
        ],
        compiler_params=params(),
        cost_estimate=cost(15.5),
        name="latent_backward",
    )(acts, *arrays, *weights, *after)


def shards(
    latents,
    pixels,
    pixel_mask,
    cotangent,
    lat_gain,
    pix_gain,
    self_gain,
    mlp_gain,
    w_query,
    w_kv,
    w_cross_out,
    w_qkv,
    w_self_out,
    w_mlp_in,
    w_mlp_out,
):
    own, group_rows, width = latents.shape
    groups, slots = pixel_mask.shape
    rows = own * group_rows
    lat_rows = latents.reshape(rows, width)
    cot_rows = cotangent.reshape(rows, width)
    pix_rows = pixels.reshape(groups * slots, width)
    gain_rows = [g.reshape(1, width) for g in (lat_gain, pix_gain, self_gain, mlp_gain)]
    lat_gain, pix_gain, self_gain, mlp_gain = gain_rows
    counts = jnp.sum(pixel_mask, axis=1, dtype=jnp.int32)
    order = orders()
    pix_here = lax.axis_index("pix").astype(jnp.int32)
    dp_here = lax.axis_index("dp").astype(jnp.int32)
    here = jnp.stack([dp_here, pix_here])

    holders = lax.axis_size("pix")
    of_holder = [
        jnp.stack([(pix_here ^ r) * own + i for i in range(own)]).astype(jnp.int32)
        for r in range(holders)
    ]
    ranked = list(range(2, holders)) + [1, 0]

    def hop(value, distance):
        pairs = [(p, p ^ distance) for p in range(holders)]
        return value if distance == 0 else lax.ppermute(value, "pix", pairs)

    lat_low, query = query_project(lat_rows, lat_gain, w_query)
    query = query.reshape(own, group_rows, width)
    queries = [hop(query, r - r % 2) for r in range(holders)]
    queries = [swap(q, CORE) if r % 2 else q for r, q in enumerate(queries)]
    pix_low, kv_rows = pix_project(pix_rows, pix_gain, w_kv, [query])
    kv = kv_rows.reshape(groups, slots, 2 * width)

    mixed = {}
    last = []
    for r in ranked:
        if r == 1:
            joined = {
                far: merge_call(mixed[far], swap(mixed[far + 1], CORE))
                for far in range(2, holders, 2)
            }
            last = list(joined.values())
        mixed[r] = cross_forward(of_holder[r], counts, queries[r], kv, last)
        last = [mixed[r]]
    parts = [mixed[0], swap(mixed[1], CORE)] + [hop(joined[far], far) for far in joined]
    parts = [part.reshape(rows, width + LANES) for part in parts]

    both_cot = (cot_rows, swap(cot_rows, CORE))
    acts, cross_stat, first, qkv, second, latents_out = latent_forward(
        parts,
        group_rows,
        lat_rows,
        cot_rows,
        self_gain,
        mlp_gain,
        (w_cross_out, w_qkv, w_self_out, w_mlp_in, w_mlp_out),
        [both_cot[1]],
    )
    grads_low, d_first, d_cross, mlp_sum, self_sum = latent_backward(
        group_rows,
        acts,
        (cot_rows, second, first, qkv, cross_stat, self_gain, mlp_gain),
        (w_mlp_in, w_self_out, w_qkv, w_cross_out),
        [],
    )
    d_cross = d_cross.reshape(own, group_rows, width + LANES)
    grads = {0: d_cross, 1: swap(d_cross, CORE)}
    for far in range(2, holders, 2):
        grads[far] = hop(d_cross, far)
        grads[far + 1] = swap(grads[far], CORE)

    both_acts = (acts, swap(acts, CORE))
    both_grads = (grads_low, swap(grads_low, CORE))
    wide = w_mlp_in.shape[1]
    low_at = 2 * wide // width
    fold = wide // width
    out_parts = weight_blocks(
        [((both_acts, wide, 0), (both_cot, width, 0))], [], here, order["yzx"], [grads_low], fold
    )
    in_parts = weight_blocks(
        [((both_acts, width, low_at), (both_acts, wide, 1))], [], here, order["zyx"], out_parts
    )
    out_steps = halvings(*out_parts, order["yzx"][:2])
    in_steps = halvings(*in_parts, order["zyx"][:2])
    mlp_parts = [jnp.concatenate(pair, axis=-1) for pair in zip(out_steps[2], in_steps[2])]
    mlp_steps = halvings(*mlp_parts, order["yzx"][2:-1])
    mlp_total = last_sum(mlp_steps[-1], order["yzx"][-1])
    self_pairs = [
        ((both_acts, width, low_at + 2), (both_grads, width, 3)),
        ((both_acts, width, low_at + 1), (both_grads, 3 * width, 0)),
        ((both_acts, width, low_at + 3), (both_grads, width, 4)),
    ]
    self_parts = weight_blocks(self_pairs, [], here, order["xyz"], in_parts)
    self_steps = halvings(*self_parts, order["xyz"][:-1])
    self_total = last_sum(self_steps[-1], order["xyz"][-1])
    dqs = {}
    d_kv, last = None, self_parts
    far_terms = []
    for far in range(2, holders, 2):
        for r in (far, far + 1):
            dqs[r], d_kv = cross_backward(
                of_holder[r], counts, queries[r], grads[r], kv, d_kv, last
            )
            last = []
        joined_dq = add_low(dqs[far], swap(dqs[far + 1], CORE))
        far_terms.append(hop(joined_dq, far))
        last = [joined_dq]
    dqs[1], d_kv = cross_backward(of_holder[1], counts, queries[1], grads[1], kv, d_kv, [])
    dqs[0], d_kv = cross_backward(of_holder[0], counts, queries[0], grads[0], kv, d_kv, last)
    near_dq = dqs[0].astype(F32) + swap(dqs[1], CORE).astype(F32)
    terms = [near_dq] + far_terms
    terms = [term.reshape(rows, width) for term in terms]
    d_kv_rows = d_kv.reshape(groups * slots, 2 * width)
    splits = [[CORE] + order["zxy"]]
    *kv_parts, kv_rows_sum = pix_weight(
        pix_low, d_kv_rows, w_kv, here, splits, [near_dq, *out_steps[1], *in_steps[1]]
    )
    kv_steps = halvings(*kv_parts, splits[0][:-1])
    kv_total = last_sum(kv_steps[-1], splits[0][-1])
    d_query, d_latents, gains = latent_end(
        terms,
        lat_rows,
        lat_gain,
        w_query,
        d_first,
        pix_gain,
        kv_rows_sum,
        (self_sum, mlp_sum),
        [*self_steps[1], *mlp_parts],
    )
    query_order = [CORE] + order["yxz"]
    query_pairs = [(((lat_low,), width, 0), ((d_query,), width, 0))]
    query_parts = weight_blocks(query_pairs, [gains], here, query_order, kv_steps[1])
    query_steps = halvings(*query_parts, query_order[:-1])
    d_pixels = pix_back(d_kv_rows, w_kv, pix_rows, pix_gain, [*query_parts, *mlp_steps[1]])
    split_at = width // holders
    sums = last_sum(query_steps[-1], query_order[-1])
    return (
        latents_out.reshape(latents.shape),
        d_latents.reshape(latents.shape),
        d_pixels.reshape(pixels.shape),
        sums[:, split_at],
        sums[:, split_at + 1],
        sums[:, split_at + 2],
        sums[:, split_at + 3],
        sums[:, :split_at],
        kv_total,
        self_total[:, 4 * split_at :],
        self_total[:, split_at : 4 * split_at],
        self_total[:, :split_at],
        mlp_total[:, fold * split_at :],
        jnp.concatenate(
            [mlp_total[:, j * split_at : (j + 1) * split_at] for j in range(fold)], axis=0
        ),
    )


def solution(mesh):
    held = P(("dp", "pix"), None, None)
    return jax.shard_map(
        shards,
        mesh=mesh,
        in_specs=(held, P("dp", "pix", None), P("dp", "pix"), held) + (P(),) * 11,
        out_specs=(held, held, P("dp", "pix", None)) + (P("dp"),) * 4 + (P("dp", "pix"),) * 7,
        check_vma=False,
    )
```
